128 devices in a mesh: dp: 16 (over z, y), code: 8 (over x, core).
Axes of the slice: x: 4, y: 4, z: 4, core: 2. Of those that a mesh axis runs over, the one named last changes fastest.
Arguments:
- vectors: float32 [65536, 256], P('dp'), may hold values from -16 to 16
- codebook: float32 [32768, 256], P('code'), may hold values from -6 to 6
- cand_blocks: int32 [64, 8, 2], P('dp', 'code'), may hold values from 0 to 3, as said below
- cand_counts: int32 [64, 8], P('dp', 'code'), may hold values from 1 to 2
Outputs:
- centroids: float32 [32768, 256], P(('code', 'dp'))
The draws below stay inside these ranges and needn't reach their ends.
Inputs may be any that keep to these rules, and one draw needn't show every extreme that they name: `cand_blocks`: within one list the first cand_counts entries are distinct.
All inputs are finite; a program needn't handle non-finite values.
Results may differ from the reference program's by a relative error of at most 0.0003.
Values sent between devices are 32-bit elements; how exact they have to be, the bound alone decides.
A program may use at most 128 MiB of HBM per device.

```python
import jax
import jax.numpy as jnp
from jax import lax

D = 256
RB = 1024
CB = 1024
CBLK_DEV = 4
SLOTS = 2
ITERS = 3
NR = 64
NCB = 32
N_CODE = 8


def draw_vectors(key, part):
    key = jax.random.fold_in(key, 37)
    total = NR * RB
    base = jnp.clip(jax.random.normal(key, (total, D), jnp.float32), -6.0, 6.0)
    index = jnp.arange(total, dtype=jnp.int32)
    picked = (index % 32 == 5).astype(jnp.float32)
    level = index // 32 % 3
    strength = jnp.where(level == 0, 0.7, jnp.where(level == 1, 1.0, 1.4)).astype(jnp.float32)
    offset = picked * strength * (40.0 / jnp.sqrt(jnp.float32(D)))
    return jnp.clip(base + offset[:, None], -16.0, 16.0).astype(jnp.float32)


def draw_cand_blocks(key, part):
    key = jax.random.fold_in(key, 11)
    scores = jax.random.randint(key, (NR, N_CODE, CBLK_DEV), 0, 1 << 20) * CBLK_DEV
    scores = scores + jnp.arange(CBLK_DEV, dtype=jnp.int32)[None, None, :]
    order = jnp.argsort(scores, axis=-1).astype(jnp.int32)
    return order[:, :, :SLOTS]


def draw_cand_counts(key, part):
    key = jax.random.fold_in(key, 23)
    first, second = jax.random.split(key)
    base = jax.random.randint(first, (1, N_CODE), 1, SLOTS + 1)
    jitter = jax.random.randint(second, (NR, N_CODE), -1, 2)
    counts = jnp.clip(base + jitter, 1, SLOTS).astype(jnp.int32)
    return counts.at[0].set(SLOTS)


def level_of(rng, dims, cuts, least, largest):
    loudness = 1.0
    for position, parts in cuts:
        heights = jax.random.uniform(jax.random.fold_in(jax.random.fold_in(rng, 6), position), (parts,), jnp.float32, least / len(cuts), largest / len(cuts))
        loudness = loudness * jnp.repeat(jnp.exp(heights), dims[position] // parts).reshape((-1,) + (1,) * (len(dims) - 1 - position))
    return loudness


def noise(stream_key, extent, spread, most, cuts=(), kind=jnp.bfloat16):
    gain = level_of(stream_key, extent, cuts, -0.22, 0.18) if cuts else 1.0
    values = jax.random.normal(stream_key, extent, jnp.float32) * spread * gain
    return jnp.minimum(jnp.maximum(values, -most), most).astype(kind)


def setup_inputs(seed: int = 0) -> dict:
    key_list = jax.random.split(jax.random.key(seed), 5)
    return {
        "vectors": draw_vectors(jax.random.fold_in(key_list[4], 71), 0),
        "codebook": noise(key_list[1], (NCB * CB, D), 1.0, 6.0, ((0, 8),), jnp.float32),
        "cand_blocks": draw_cand_blocks(jax.random.fold_in(key_list[4], 71), 0),
        "cand_counts": draw_cand_counts(jax.random.fold_in(key_list[4], 71), 0),
    }


TEMPER = 4.0
SLACK = 3.0


def reference(vectors, codebook, cand_blocks, cand_counts):
    rows = vectors.reshape(NR, RB, D)
    books = codebook.reshape(NCB, CB, D)
    owners = jnp.arange(N_CODE, dtype=jnp.int32)[:, None] * CBLK_DEV
    gblocks = (cand_blocks + owners[None]).reshape(NR, N_CODE * SLOTS).astype(jnp.int32)
    valid = (jnp.arange(SLOTS, dtype=jnp.int32)[None, None, :] < cand_counts[:, :, None]).reshape(NR, N_CODE * SLOTS)

    def tile_cost(index):
        xrow = rows[index]
        picked = books[gblocks[index]]
        dots = jnp.einsum('id,tcd->tic', xrow, picked, precision=lax.Precision.HIGHEST)
        return (jnp.sum(xrow * xrow, -1)[None, :, None] + jnp.sum(picked * picked, -1)[:, None, :] - 2.0 * dots) / TEMPER

    potential_v = jnp.zeros((NCB, CB), jnp.float32)
    potential_u = jnp.zeros((NR, RB), jnp.float32)
    for step in range(ITERS):
        def row_pass(index):
            cost = tile_cost(index)
            score = potential_v[gblocks[index]][:, None, :] - cost
            score = jnp.where(valid[index][:, None, None], score, -jnp.inf)
            peak = jnp.max(score, axis=(0, 2))
            total = jnp.sum(jnp.exp(score - peak[None, :, None]), axis=(0, 2))
            return -(peak + jnp.log(total))

        potential_u = lax.map(row_pass, jnp.arange(NR, dtype=jnp.int32))

        def col_step(carry, index):
            peaks, masses = carry
            cost = tile_cost(index)
            shifted = potential_u[index][None, :, None] - cost
            tile_top = jnp.where(valid[index][:, None], jnp.max(shifted, axis=1), -jnp.inf)
            blocks = gblocks[index]
            old_top = peaks[blocks]
            new_top = jnp.maximum(old_top, tile_top)
            expo = jnp.where(valid[index][:, None, None], jnp.exp(shifted - new_top[:, None, :]), 0.0)
            new_mass = masses[blocks] * jnp.exp(old_top - new_top) + jnp.sum(expo, axis=1)
            return (peaks.at[blocks].set(new_top), masses.at[blocks].set(new_mass)), None

        start = (jnp.full((NCB, CB), -SLACK, jnp.float32), jnp.zeros((NCB, CB), jnp.float32))
        (peaks, masses), unused = lax.scan(col_step, start, jnp.arange(NR, dtype=jnp.int32))
        potential_v = -(peaks + jnp.log(masses + jnp.exp(-SLACK - peaks)))

    def sum_step(sums, index):
        cost = tile_cost(index)
        blocks = gblocks[index]
        weight = jnp.exp(potential_u[index][None, :, None] + potential_v[blocks][:, None, :] - cost)
        weight = jnp.where(valid[index][:, None, None], weight, 0.0)
        contrib = jnp.einsum('tic,id->tcd', weight, rows[index], precision=lax.Precision.HIGHEST)
        return sums.at[blocks].add(contrib), None

    sums, unused = lax.scan(sum_step, jnp.zeros((NCB, CB, D), jnp.float32), jnp.arange(NR, dtype=jnp.int32))
    result = sums + jnp.exp(potential_v - SLACK)[:, :, None] * books
    return result.reshape(NCB * CB, D)
```

```python
import functools
import math

import jax
import jax.numpy as jnp
from jax import lax
from jax.experimental import pallas as pl
from jax.experimental.pallas import tpu as pltpu
from jax.sharding import PartitionSpec as P

MESH = pl.DeviceIdType.MESH
LOG2E = 1.0 / math.log(2.0)
EPS = math.exp(-3.0)
F32 = jnp.float32
BF16 = jnp.bfloat16
NT = (((1,), (1,)), ((), ()))


def split(v):
    hi = v.astype(BF16)
    return hi, (v - hi.astype(F32)).astype(BF16)


def repeat8(a):
    return jnp.concatenate([a] * 8, axis=1)


def wait_bytes(ref, sem):
    pltpu.make_async_copy(ref, ref, sem).wait()


def kernel(
    blocks, counts, x_ref, c_hbm, out_ref,
    e, s, ccat, bias, arep, prod, cown,
    rg0, rg, alpha, gvec, cols, zg, yg, msum, y1, z1, u0, u1,
    c_sem, r_send, r_recv, d_send, d_recv, p_send, p_recv,
):
    dp = lax.axis_index("dp")
    code = lax.axis_index("code")
    z, y = dp // 4, dp % 4

    def code_peer(d):
        return (dp, (code + d) % 8)

    def z_peer(d):
        return (((z + d) % 4) * 4 + y, code)

    def y_peer(d):
        return (z * 4 + (y + d) % 4, code)

    def push(src, dst, send, recv, peer):
        pltpu.make_async_remote_copy(
            src_ref=src, dst_ref=dst, send_sem=send, recv_sem=recv,
            device_id=peer, device_id_type=MESH,
        ).start()

    for h in range(2):
        for p in range(4):
            for q in range(4):
                pltpu.make_async_copy(
                    c_hbm.at[:, q, p, :, pl.ds(h * 128, 128)],
                    s.at[h, :, p, pl.ds(q * 64, 64), :],
                    c_sem.at[0],
                ).start()
    own_copy = pltpu.make_async_copy(c_hbm.at[z, y], cown, c_sem.at[1])
    own_copy.start()

    barrier = pltpu.get_barrier_semaphore()
    for d in range(1, 8):
        pl.semaphore_signal(barrier, inc=1, device_id=code_peer(d), device_id_type=MESH)
    for d in range(1, 4):
        pl.semaphore_signal(barrier, inc=1, device_id=z_peer(d), device_id_type=MESH)
        pl.semaphore_signal(barrier, inc=1, device_id=y_peer(d), device_id_type=MESH)

    wait_bytes(s, c_sem.at[0])

    def prepare(n, carry):
        b, p = n // 4, n % 4
        c0 = s[0, b, p]
        c1 = s[1, b, p]
        norm = jnp.sum(c0 * c0 + c1 * c1, axis=1, keepdims=True) * (-0.25 * LOG2E)
        rows = pl.ds(pl.multiple_of(p * 256, 256), 256)
        bias[b, rows, :] = jnp.broadcast_to(norm, (256, 128))
        for h, part in enumerate((c0, c1)):
            hi, lo = split(part * (0.5 * LOG2E))
            ccat[b, rows, h * 128:(h + 1) * 128] = hi
            ccat[b, rows, 256 + h * 128:256 + (h + 1) * 128] = lo
        return carry

    lax.fori_loop(0, 16, prepare, 0)

    def stage(n, carry):
        r, iq = n // 4, n % 4
        rows = pl.ds(pl.multiple_of(n * 256, 256), 256)
        cols_i = pl.ds(pl.multiple_of(iq * 256, 256), 256)
        xh, xl = split(x_ref[rows, :])
        xcat = jnp.concatenate([xh, xl, xh], axis=1)
        top = None
        for slot in range(2):
            b = blocks[r, slot]
            ch = ccat[b, :, 0:256]
            cl = ccat[b, :, 256:512]
            lhs = jnp.concatenate([ch, ch, cl], axis=1)
            score = lax.dot_general(lhs, xcat, NT, preferred_element_type=F32)
            bb = bias[b]
            score = score + jnp.concatenate([bb, bb], axis=1)
            e[r * 2 + slot, :, cols_i] = score
            peak = jnp.max(score, axis=0, keepdims=True)
            if slot == 0:
                top = peak
            else:
                top = jnp.where(counts[r] > 1, jnp.maximum(top, peak), top)
        total = jnp.zeros((8, 256), F32)
        for slot in range(2):
            shift = top if slot == 0 else jnp.where(counts[r] > 1, top, 3e38)
            w = jnp.exp2(e[r * 2 + slot, :, cols_i] - shift)
            e[r * 2 + slot, :, cols_i] = w
            total = total + jnp.sum(w.reshape(128, 8, 256), axis=0)
        rg0[r, code, :, cols_i] = top
        rg0[r, code, :, pl.ds(pl.multiple_of(1024 + iq * 256, 256), 256)] = jnp.sum(
            total, axis=0, keepdims=True
        )
        return carry

    def row_first(r, carry):
        lax.fori_loop(r * 4, r * 4 + 4, stage, 0)

        @pl.when(r == 0)
        def _():
            pl.semaphore_wait(barrier, 13)

        for d in range(1, 8):
            push(rg0.at[r, code], rg0.at[r, code], r_send.at[0, r], r_recv.at[0, r], code_peer(d))
        return carry

    lax.fori_loop(0, 4, row_first, 0)

    def col_block(r):
        g = repeat_rows(gvec[r])
        for slot in range(2):
            def chunk(n, carry):
                k = pl.ds(pl.multiple_of(n * 128, 128), 128)
                w = e[r * 2 + slot, k, :] * g
                acc = w[:, 0:128]
                for j in range(1, 8):
                    acc = acc + w[:, j * 128:(j + 1) * 128]
                cols[r * 2 + slot, :, k] = jnp.sum(acc.T, axis=0, keepdims=True)
                return carry

            lax.fori_loop(0, 8, chunk, 0)

    def repeat_rows(v):
        return jnp.broadcast_to(v, (128, 1024))

    def col_first(r, carry):
        wait_bytes(rg0.at[r, pl.ds(0, 7)], r_recv.at[0, r])
        tops = [rg0[r, j, :, 0:1024] for j in range(8)]
        best = functools.reduce(jnp.maximum, tops)
        total = jnp.zeros((1, 1024), F32)
        for j in range(8):
            total = total + jnp.exp2(tops[j] - best) * rg0[r, j, :, 1024:2048]
        mine = jnp.exp2(rg0[r, code, :, 0:1024] - best)
        alpha[r] = mine
        gvec[r] = mine / total
        col_block(r)
        return carry

    def col_next(it):
        def body(r, carry):
            wait_bytes(rg.at[it, r, pl.ds(0, 7)], r_recv.at[it + 1, r])
            total = rg[it, r, 0]
            for j in range(1, 8):
                total = total + rg[it, r, j]
            gvec[r] = alpha[r] / total
            col_block(r)
            return carry

        return body

    def row_next(it):
        def body(r, carry):
            acc = jnp.zeros((8, 1024), F32)
            for slot in range(2):
                b = blocks[r, slot]

                def chunk(n, acc):
                    k = pl.ds(pl.multiple_of(n * 64, 64), 64)
                    w = e[r * 2 + slot, k, :] * repeat8(arep[b, k, :])
                    return acc + jnp.sum(w.reshape(8, 8, 1024), axis=0)

                acc = lax.fori_loop(0, 16, chunk, acc)
            rg[it, r, code] = jnp.sum(acc, axis=0, keepdims=True) * alpha[r]
            for d in range(1, 8):
                push(
                    rg.at[it, r, code], rg.at[it, r, code],
                    r_send.at[it + 1, r], r_recv.at[it + 1, r], code_peer(d),
                )
            return carry

        return body

    def has_slot(r, b):
        second = (blocks[r, 1] == b) & (counts[r] > 1)
        slot = jnp.where(second, 1, 0)
        has = second | (blocks[r, 0] == b)
        return has, slot

    def dp_sum(it):
        for b in range(4):
            total = jnp.zeros((1, 1024), F32)
            for r in range(4):
                has, slot = has_slot(r, b)
                total = total + jnp.where(has, cols[r * 2 + slot], 0.0)
            zg[it, z, b] = total
        for d in range(1, 4):
            push(zg.at[it, z], zg.at[it, z], d_send.at[0, it], d_recv.at[0, it], z_peer(d))

    def dp_mid(it):
        wait_bytes(zg.at[it, pl.ds(0, 3)], d_recv.at[0, it])
        for b in range(4):
            yg[it, y, b] = (zg[it, 0, b] + zg[it, 1, b]) + (zg[it, 2, b] + zg[it, 3, b])
        for d in range(1, 4):
            push(yg.at[it, y], yg.at[it, y], d_send.at[1, it], d_recv.at[1, it], y_peer(d))

    def dp_end(it):
        wait_bytes(yg.at[it, pl.ds(0, 3)], d_recv.at[1, it])
        for b in range(4):
            msum[b] = (yg[it, 0, b] + yg[it, 1, b]) + (yg[it, 2, b] + yg[it, 3, b])

    def spread(v):
        return jnp.broadcast_to(v, (128, 128)).T

    def next_a(it):
        dp_sum(it)
        dp_mid(it)
        dp_end(it)
        for b in range(4):
            msum[b] = 1.0 / (msum[b] + EPS)

        def lay(n, carry):
            b, j = n // 8, n % 8
            k = pl.ds(pl.multiple_of(j * 128, 128), 128)
            arep[b, k, :] = spread(msum[b, :, k])
            return carry

        lax.fori_loop(0, 32, lay, 0)

    lax.fori_loop(0, 4, col_first, 0)
    next_a(0)
    lax.fori_loop(0, 4, row_next(0), 0)
    lax.fori_loop(0, 4, col_next(0), 0)
    next_a(1)
    lax.fori_loop(0, 4, row_next(1), 0)
    lax.fori_loop(0, 4, col_next(1), 0)
    dp_sum(2)

    def scale(n, carry):
        r, j = n // 8, n % 8
        i = pl.ds(pl.multiple_of(j * 128, 128), 128)
        gr = spread(gvec[r, :, i])
        xs = x_ref[pl.ds(pl.multiple_of(n * 128, 128), 128), :] * jnp.concatenate([gr, gr], axis=1)
        hi, lo = split(xs)
        ccat[r, i, 0:256] = hi
        ccat[r, i, 256:512] = lo
        return carry

    lax.fori_loop(0, 32, scale, 0)
    dp_mid(2)

    def reduce_first(p):
        wait_bytes(y1.at[:, p], p_recv.at[0, p])
        wait_bytes(z1.at[:, p], p_recv.at[1, p])
        own = pl.ds(pl.multiple_of(y * 64, 64), 64)
        for b in range(4):
            s[0, b, p, own, :] = (s[0, b, p, own, :] + y1[0, p, b]) + (y1[1, p, b] + y1[2, p, b])
        s[1, z, p] = (s[1, z, p] + z1[0, p]) + (z1[1, p] + z1[2, p])
        for d in range(1, 4):
            push(s.at[0, (z + d) % 4, p, own, :], u0.at[d - 1, p], p_send.at[2, p], p_recv.at[2, p], z_peer(d))
            dest = pl.ds(pl.multiple_of(((y + d) % 4) * 64, 64), 64)
            push(s.at[1, z, p, dest, :], u1.at[d - 1, p], p_send.at[3, p], p_recv.at[3, p], y_peer(d))

    def part(p, carry):
        rows = pl.ds(pl.multiple_of(p * 256, 256), 256)

        def one(r, carry):
            xh = ccat[r, :, 0:256]
            xl = ccat[r, :, 256:512]
            rhs = jnp.concatenate([xh, xl, xh], axis=0)
            for slot in range(2):
                eh, el = split(e[r * 2 + slot, rows, :])
                lhs = jnp.concatenate([eh, eh, el], axis=1)
                prod[r * 2 + slot] = jnp.dot(lhs, rhs, preferred_element_type=F32)
            return carry

        lax.fori_loop(0, 4, one, 0)
        for b in range(4):
            total = jnp.zeros((256, 256), F32)
            for r in range(4):
                has, slot = has_slot(r, b)
                total = total + jnp.where(has, prod[r * 2 + slot], 0.0)
            s[0, b, p] = total[:, 0:128]
            s[1, b, p] = total[:, 128:256]
        for d in range(1, 4):
            dest = pl.ds(pl.multiple_of(((y + d) % 4) * 64, 64), 64)
            push(s.at[0, :, p, dest, :], y1.at[d - 1, p], p_send.at[0, p], p_recv.at[0, p], y_peer(d))
            push(s.at[1, (z + d) % 4, p], z1.at[d - 1, p], p_send.at[1, p], p_recv.at[1, p], z_peer(d))

        @pl.when(p > 0)
        def _():
            reduce_first(p - 1)

        return carry

    lax.fori_loop(0, 4, part, 0)
    dp_end(2)
    own_copy.wait()

    def lay_own(j, carry):
        k = pl.ds(pl.multiple_of(j * 128, 128), 128)
        arep[0, k, :] = spread(1.0 / (msum[z, :, k] + EPS))
        return carry

    lax.fori_loop(0, 8, lay_own, 0)
    reduce_first(3)

    def finish(p, carry):
        wait_bytes(u0.at[:, p], p_recv.at[2, p])
        wait_bytes(u1.at[:, p], p_recv.at[3, p])
        own = pl.ds(pl.multiple_of(y * 64, 64), 64)
        f0 = (s[0, z, p, own, :] + u0[0, p]) + (u0[1, p] + u0[2, p])
        f1 = (s[1, z, p, own, :] + u1[0, p]) + (u1[1, p] + u1[2, p])
        a = arep[0, pl.ds(pl.multiple_of(p * 256 + y * 64, 64), 64), :]
        out_ref[p, :, 0:128] = (f0 + EPS * cown[p, :, 0:128]) * a
        out_ref[p, :, 128:256] = (f1 + EPS * cown[p, :, 128:256]) * a
        return carry

    lax.fori_loop(0, 4, finish, 0)

    def drain_rows(r, carry):
        wait_bytes(rg0.at[r, pl.ds(0, 7)], r_send.at[0, r])
        wait_bytes(rg.at[0, r, pl.ds(0, 7)], r_send.at[1, r])
        wait_bytes(rg.at[1, r, pl.ds(0, 7)], r_send.at[2, r])
        wait_bytes(y1.at[:, r], p_send.at[0, r])
        wait_bytes(z1.at[:, r], p_send.at[1, r])
        wait_bytes(u0.at[:, r], p_send.at[2, r])
        wait_bytes(u1.at[:, r], p_send.at[3, r])
        return carry

    lax.fori_loop(0, 4, drain_rows, 0)
    for it in range(3):
        wait_bytes(zg.at[it, pl.ds(0, 3)], d_send.at[0, it])
        wait_bytes(yg.at[it, pl.ds(0, 3)], d_send.at[1, it])


def local(vectors, codebook, cand_blocks, cand_counts):
    smem = pl.BlockSpec(memory_space=pltpu.SMEM)
    vmem = pl.BlockSpec(memory_space=pltpu.VMEM)
    out = pl.pallas_call(
        kernel,
        out_shape=jax.ShapeDtypeStruct((4, 64, 256), F32),
        in_specs=[smem, smem, vmem, pl.BlockSpec(memory_space=pl.ANY)],
        out_specs=vmem,
        scratch_shapes=[
            pltpu.VMEM((8, 1024, 1024), F32),
            pltpu.VMEM((2, 4, 4, 256, 128), F32),
            pltpu.VMEM((4, 1024, 512), BF16),
            pltpu.VMEM((4, 1024, 128), F32),
            pltpu.VMEM((4, 1024, 128), F32),
            pltpu.VMEM((8, 256, 256), F32),
            pltpu.VMEM((4, 64, 256), F32),
            pltpu.VMEM((4, 8, 1, 2048), F32),
            pltpu.VMEM((2, 4, 8, 1, 1024), F32),
            pltpu.VMEM((4, 1, 1024), F32),
            pltpu.VMEM((4, 1, 1024), F32),
            pltpu.VMEM((8, 1, 1024), F32),
            pltpu.VMEM((3, 4, 4, 1, 1024), F32),
            pltpu.VMEM((3, 4, 4, 1, 1024), F32),
            pltpu.VMEM((4, 1, 1024), F32),
            pltpu.VMEM((3, 4, 4, 64, 128), F32),
            pltpu.VMEM((3, 4, 256, 128), F32),
            pltpu.VMEM((3, 4, 64, 128), F32),
            pltpu.VMEM((3, 4, 64, 128), F32),
            pltpu.SemaphoreType.DMA((2,)),
            pltpu.SemaphoreType.DMA((3, 4)),
            pltpu.SemaphoreType.DMA((3, 4)),
            pltpu.SemaphoreType.DMA((2, 3)),
            pltpu.SemaphoreType.DMA((2, 3)),
            pltpu.SemaphoreType.DMA((4, 4)),
            pltpu.SemaphoreType.DMA((4, 4)),
        ],
        compiler_params=pltpu.CompilerParams(
            collective_id=0, has_side_effects=True, vmem_limit_bytes=63 * 1024 * 1024,
        ),
    )(
        cand_blocks.reshape(4, 2),
        cand_counts.reshape(4),
        vectors,
        codebook.reshape(4, 4, 4, 64, 256),
    )
    return out.reshape(256, 256)


def solution(mesh):
    return jax.shard_map(
        local,
        mesh=mesh,
        in_specs=(P("dp", None), P("code", None), P("dp", "code", None), P("dp", "code")),
        out_specs=P(("code", "dp"), None),
        check_vma=False,
    )
```

```python
import functools
import math

import jax
import jax.numpy as jnp
from jax import lax
from jax.experimental import pallas as pl
from jax.experimental.pallas import tpu as pltpu
from jax.sharding import PartitionSpec as P

MESH = pl.DeviceIdType.MESH
LOG2E = 1.0 / math.log(2.0)
EPS = math.exp(-3.0)
F32 = jnp.float32
BF16 = jnp.bfloat16
MCH = 1024
NT = (((1,), (1,)), ((), ()))


def split(v):
    hi = v.astype(BF16)
    return hi, (v - hi.astype(F32)).astype(BF16)


def repeat8(a):
    return jnp.concatenate([a] * 8, axis=1)


def spread(v):
    return jnp.broadcast_to(v, (128, 128)).T


def wait_bytes(ref, sem):
    pltpu.make_async_copy(ref, ref, sem).wait()


def kernel(
    blocks, counts, x_hbm, c_hbm, out_ref,
    e, s, ccat, xcat, bias, arep, raw0, raw1, cown,
    rg0, rg, alpha, gvec, dg, mg, mrep, y1, z1, u0, u1,
    c_sem, r_send, r_recv, d_send, d_recv, m_send, m_recv, p_send, p_recv,
):
    dp = lax.axis_index("dp")
    code = lax.axis_index("code")
    z, y = dp // 4, dp % 4
    raws = (raw0, raw1)

    def code_peer(d):
        return (dp, (code + d) % 8)

    def dp_peer(d):
        return ((dp + d) % 16, code)

    def z_peer(d):
        return (((z + d) % 4) * 4 + y, code)

    def y_peer(d):
        return (z * 4 + (y + d) % 4, code)

    def push(src, dst, send, recv, peer):
        pltpu.make_async_remote_copy(
            src_ref=src, dst_ref=dst, send_sem=send, recv_sem=recv,
            device_id=peer, device_id_type=MESH,
        ).start()

    for h in range(2):
        for p in range(4):
            for q in range(4):
                pltpu.make_async_copy(
                    c_hbm.at[:, q, p, :, pl.ds(h * 128, 128)],
                    s.at[h, :, p, pl.ds(q * 64, 64), :],
                    c_sem.at[0],
                ).start()
    for r in range(4):
        pltpu.make_async_copy(x_hbm.at[r], e.at[7, :, pl.ds(r * 256, 256)], c_sem.at[1]).start()
    own_copy = pltpu.make_async_copy(c_hbm.at[z, y], cown, c_sem.at[2])
    own_copy.start()

    barrier = pltpu.get_barrier_semaphore()
    for d in range(1, 8):
        pl.semaphore_signal(barrier, inc=1, device_id=code_peer(d), device_id_type=MESH)
    for d in range(1, 16):
        pl.semaphore_signal(barrier, inc=1, device_id=dp_peer(d), device_id_type=MESH)

    wait_bytes(s, c_sem.at[0])

    def prepare(n, carry):
        b, p = n // 4, n % 4
        c0 = s[0, b, p]
        c1 = s[1, b, p]
        norm = jnp.sum(c0 * c0 + c1 * c1, axis=1, keepdims=True) * (-0.25 * LOG2E)
        rows = pl.ds(pl.multiple_of(p * 256, 256), 256)
        bias[b, rows, :] = jnp.broadcast_to(norm, (256, 128))
        for h, part in enumerate((c0, c1)):
            hi, lo = split(part * (0.5 * LOG2E))
            ccat[b, rows, h * 128:(h + 1) * 128] = hi
            ccat[b, rows, 256 + h * 128:256 + (h + 1) * 128] = lo
        return carry

    lax.fori_loop(0, 16, prepare, 0)
    wait_bytes(e.at[7], c_sem.at[1])

    def score(r, iq):
        raw = raws[iq % 2]
        lanes = slice(iq * 256, (iq + 1) * 256)
        xs = e[7, lanes, pl.ds(pl.multiple_of(r * 256, 256), 256)]
        xh, xl = split(xs)
        xcat[r, lanes, 0:256] = xh
        xcat[r, lanes, 256:512] = xl
        rhs = jnp.concatenate([xh, xl, xh], axis=1)
        top = None
        for slot in range(2):
            b = blocks[r, 0, slot]
            peak = None
            for k in range(0, 1024, MCH):
                rows = slice(k, k + MCH)
                ch = ccat[b, rows, 0:256]
                cl = ccat[b, rows, 256:512]
                lhs = jnp.concatenate([ch, ch, cl], axis=1)
                bb = bias[b, rows, :]
                value = lax.dot_general(lhs, rhs, NT, preferred_element_type=F32)
                value = value + jnp.concatenate([bb, bb], axis=1)
                raw[slot * 4 + k // 256:slot * 4 + (k + MCH) // 256] = value.reshape(MCH // 256, 256, 256)
                peak_k = jnp.max(value.reshape(MCH // 8, 8, 256), axis=0)
                peak = peak_k if peak is None else jnp.maximum(peak, peak_k)
            peak = jnp.max(peak, axis=0, keepdims=True)
            if slot == 0:
                top = peak
            else:
                top = jnp.where(counts[r, 0] > 1, jnp.maximum(top, peak), top)
        rg0[r, code, :, lanes] = top

    def expo(r, iq):
        raw = raws[iq % 2]
        lanes = slice(iq * 256, (iq + 1) * 256)
        top = rg0[r, code, :, lanes]
        total = jnp.zeros((8, 256), F32)
        for slot in range(2):
            shift = top if slot == 0 else jnp.where(counts[r, 0] > 1, top, 3e38)
            for k in range(0, 1024, 256):
                rows = slice(k, k + 256)
                w = jnp.exp2(raw[slot * 4 + k // 256] - shift)
                e[r * 2 + slot, rows, lanes] = w
                total = total + jnp.sum(w.reshape(32, 8, 256), axis=0)
        rg0[r, code, :, 1024 + iq * 256:1280 + iq * 256] = jnp.sum(total, axis=0, keepdims=True)

    def send_first(r):
        for d in range(1, 8):
            push(rg0.at[r, code], rg0.at[r, code], r_send.at[0, r], r_recv.at[0, r], code_peer(d))

    score(0, 0)

    def row_first(r, carry):
        for iq in range(3):
            score(r, iq + 1)
            expo(r, iq)

        @pl.when(r == 0)
        def _():
            pl.semaphore_wait(barrier, 22)

        score(r + 1, 0)
        expo(r, 3)
        send_first(r)
        return carry

    lax.fori_loop(0, 3, row_first, 0)
    for iq in range(3):
        score(3, iq + 1)
        expo(3, iq)
    expo(3, 3)
    send_first(3)

    def col_block(r):
        g = gvec[r]
        for slot in range(2):
            def chunk(n, carry):
                k = pl.ds(pl.multiple_of(n * 256, 256), 256)
                w = e[r * 2 + slot, k, :] * g
                acc = w[:, 0:128]
                for j in range(1, 8):
                    acc = acc + w[:, j * 128:(j + 1) * 128]
                s[r // 2, (r % 2) * 2 + slot, n] = acc
                return carry

            lax.fori_loop(0, 4, chunk, 0)

    def col_first(r, carry):
        wait_bytes(rg0.at[r, pl.ds(0, 7)], r_recv.at[0, r])
        tops = [rg0[r, j, :, 0:1024] for j in range(8)]
        best = functools.reduce(jnp.maximum, tops)
        total = jnp.zeros((1, 1024), F32)
        for j in range(8):
            total = total + jnp.exp2(tops[j] - best) * rg0[r, j, :, 1024:2048]
        mine = jnp.exp2(rg0[r, code, :, 0:1024] - best)
        alpha[r] = mine
        gvec[r] = mine / total
        col_block(r)
        return carry

    def factor(it, r):
        wait_bytes(rg.at[it, r, pl.ds(0, 7)], r_recv.at[it + 1, r])
        total = rg[it, r, 0]
        for j in range(1, 8):
            total = total + rg[it, r, j]
        gvec[r] = alpha[r] / total

    def col_next(r, carry):
        factor(0, r)
        col_block(r)
        return carry

    def row_next(it):
        def body(r, carry):
            acc = jnp.zeros((8, 1024), F32)
            for slot in range(2):
                b = blocks[r, 0, slot]

                def chunk(n, acc):
                    k = pl.ds(pl.multiple_of(n * 64, 64), 64)
                    w = e[r * 2 + slot, k, :] * repeat8(arep[b, k, :])
                    return acc + jnp.sum(w.reshape(8, 8, 1024), axis=0)

                acc = lax.fori_loop(0, 16, chunk, acc)
            rg[it, r, code] = jnp.sum(acc, axis=0, keepdims=True) * alpha[r]
            for d in range(1, 8):
                push(
                    rg.at[it, r, code], rg.at[it, r, code],
                    r_send.at[it + 1, r], r_recv.at[it + 1, r], code_peer(d),
                )
            return carry

        return body

    def has_slot(r, b):
        second = (blocks[r, 0, 1] == b) & (counts[r, 0] > 1)
        slot = jnp.where(second, 1, 0)
        has = second | (blocks[r, 0, 0] == b)
        return has, slot

    def next_a(it):
        def gather(b, carry):
            for p in range(4):
                total = jnp.zeros((256, 128), F32)
                for r in range(4):
                    has, slot = has_slot(r, b)
                    total = total + jnp.where(has, s[r // 2, (r % 2) * 2 + slot, p], 0.0)
                for j in range(2):
                    row = jnp.sum(total[j * 128:(j + 1) * 128, :].T, axis=0, keepdims=True)
                    dg[it, dp, pl.ds(b * 8 + p * 2 + j, 1), :] = row
            return carry

        lax.fori_loop(0, 4, gather, 0)
        for d in range(1, 16):
            push(dg.at[it, dp], dg.at[it, dp], d_send.at[it], d_recv.at[it], dp_peer(d))
        wait_bytes(dg.at[it, pl.ds(0, 15)], d_recv.at[it])
        total = dg[it, 0]
        for j in range(1, 16):
            total = total + dg[it, j]
        mrep[0, 0:32, :] = 1.0 / (total + EPS)

        def lay(b, carry):
            for j in range(8):
                arep[b, j * 128:(j + 1) * 128, :] = spread(mrep[0, pl.ds(b * 8 + j, 1), :])
            return carry

        lax.fori_loop(0, 4, lay, 0)

    lax.fori_loop(0, 4, col_first, 0)
    next_a(0)
    lax.fori_loop(0, 4, row_next(0), 0)
    lax.fori_loop(0, 4, col_next, 0)
    next_a(1)
    lax.fori_loop(0, 4, row_next(1), 0)

    def last_factor(r, carry):
        factor(1, r)
        return carry

    lax.fori_loop(0, 4, last_factor, 0)

    def reduce_first(p):
        wait_bytes(y1.at[:, p], p_recv.at[0, p])
        wait_bytes(z1.at[:, p], p_recv.at[1, p])
        own = pl.ds(pl.multiple_of(y * 64, 64), 64)
        for b in range(4):
            s[0, b, p, own, :] = (s[0, b, p, own, :] + y1[0, p, b]) + (y1[1, p, b] + y1[2, p, b])
        s[1, z, p] = (s[1, z, p] + z1[0, p]) + (z1[1, p] + z1[2, p])
        for d in range(1, 4):
            push(s.at[0, (z + d) % 4, p, own, :], u0.at[d - 1, p], p_send.at[2, p], p_recv.at[2, p], z_peer(d))
            dest = pl.ds(pl.multiple_of(((y + d) % 4) * 64, 64), 64)
            push(s.at[1, z, p, dest, :], u1.at[d - 1, p], p_send.at[3, p], p_recv.at[3, p], y_peer(d))

    def part(p, carry):
        rows = pl.ds(pl.multiple_of(p * 256, 256), 256)

        def one(r, carry):
            xh = xcat[r, :, 0:256]
            xl = xcat[r, :, 256:512]
            rhs = jnp.concatenate([xh, xl, xh], axis=0)
            g = gvec[r]
            for slot in range(2):
                w = e[r * 2 + slot, rows, :] * g
                acc = w[:, 0:128]
                for j in range(1, 8):
                    acc = acc + w[:, j * 128:(j + 1) * 128]
                t = r * 2 + slot
                raw1[t, :, 0:128] = acc
                eh, el = split(w)
                lhs = jnp.concatenate([eh, eh, el], axis=1)
                raw0[t] = jnp.dot(lhs, rhs, preferred_element_type=F32)
            return carry

        lax.fori_loop(0, 4, one, 0)
        for b in range(4):
            total = jnp.zeros((256, 256), F32)
            mass = jnp.zeros((256, 128), F32)
            for r in range(4):
                has, slot = has_slot(r, b)
                total = total + jnp.where(has, raw0[r * 2 + slot], 0.0)
                mass = mass + jnp.where(has, raw1[r * 2 + slot, :, 0:128], 0.0)
            s[0, b, p] = total[:, 0:128]
            s[1, b, p] = total[:, 128:256]
            for j in range(2):
                mg[p, dp, b * 2 + j:b * 2 + j + 1, :] = jnp.sum(
                    mass[j * 128:(j + 1) * 128, :].T, axis=0, keepdims=True
                )
        for d in range(1, 4):
            dest = pl.ds(pl.multiple_of(((y + d) % 4) * 64, 64), 64)
            push(s.at[0, :, p, dest, :], y1.at[d - 1, p], p_send.at[0, p], p_recv.at[0, p], y_peer(d))
            push(s.at[1, (z + d) % 4, p], z1.at[d - 1, p], p_send.at[1, p], p_recv.at[1, p], z_peer(d))
        for d in range(1, 16):
            push(mg.at[p, dp], mg.at[p, dp], m_send.at[p], m_recv.at[p], dp_peer(d))

        @pl.when(p > 0)
        def _():
            reduce_first(p - 1)

        return carry

    lax.fori_loop(0, 4, part, 0)
    own_copy.wait()
    reduce_first(3)

    def finish(p, carry):
        wait_bytes(mg.at[p, pl.ds(0, 15)], m_recv.at[p])
        mass = mg[p, 0]
        for j in range(1, 16):
            mass = mass + mg[p, j]
        mrep[1, 0:8, :] = 1.0 / (mass + EPS)
        mrep[0] = spread(mrep[1, pl.ds(z * 2 + y // 2, 1), :])
        a = mrep[0, pl.ds(pl.multiple_of((y % 2) * 64, 64), 64), :]
        wait_bytes(u0.at[:, p], p_recv.at[2, p])
        wait_bytes(u1.at[:, p], p_recv.at[3, p])
        own = pl.ds(pl.multiple_of(y * 64, 64), 64)
        f0 = (s[0, z, p, own, :] + u0[0, p]) + (u0[1, p] + u0[2, p])
        f1 = (s[1, z, p, own, :] + u1[0, p]) + (u1[1, p] + u1[2, p])
        out_ref[p, :, 0:128] = (f0 + EPS * cown[p, :, 0:128]) * a
        out_ref[p, :, 128:256] = (f1 + EPS * cown[p, :, 128:256]) * a
        return carry

    lax.fori_loop(0, 4, finish, 0)

    def drain_rows(r, carry):
        wait_bytes(rg0.at[r, pl.ds(0, 7)], r_send.at[0, r])
        wait_bytes(rg.at[0, r, pl.ds(0, 7)], r_send.at[1, r])
        wait_bytes(rg.at[1, r, pl.ds(0, 7)], r_send.at[2, r])
        wait_bytes(mg.at[r, pl.ds(0, 15)], m_send.at[r])
        wait_bytes(y1.at[:, r], p_send.at[0, r])
        wait_bytes(z1.at[:, r], p_send.at[1, r])
        wait_bytes(u0.at[:, r], p_send.at[2, r])
        wait_bytes(u1.at[:, r], p_send.at[3, r])
        return carry

    lax.fori_loop(0, 4, drain_rows, 0)
    for it in range(2):
        wait_bytes(dg.at[it, pl.ds(0, 15)], d_send.at[it])


def local(vectors, codebook, cand_blocks, cand_counts):
    smem = pl.BlockSpec(memory_space=pltpu.SMEM)
    hbm = pl.BlockSpec(memory_space=pl.ANY)
    out = pl.pallas_call(
        kernel,
        out_shape=jax.ShapeDtypeStruct((4, 64, 256), F32),
        in_specs=[smem, smem, hbm, hbm],
        out_specs=pl.BlockSpec(memory_space=pltpu.VMEM),
        scratch_shapes=[
            pltpu.VMEM((8, 1024, 1024), F32),
            pltpu.VMEM((2, 4, 4, 256, 128), F32),
            pltpu.VMEM((4, 1024, 512), BF16),
            pltpu.VMEM((4, 1024, 512), BF16),
            pltpu.VMEM((4, 1024, 128), F32),
            pltpu.VMEM((4, 1024, 128), F32),
            pltpu.VMEM((8, 256, 256), F32),
            pltpu.VMEM((8, 256, 256), F32),
            pltpu.VMEM((4, 64, 256), F32),
            pltpu.VMEM((4, 8, 1, 2048), F32),
            pltpu.VMEM((2, 4, 8, 1, 1024), F32),
            pltpu.VMEM((4, 1, 1024), F32),
            pltpu.VMEM((4, 1, 1024), F32),
            pltpu.VMEM((2, 16, 32, 128), F32),
            pltpu.VMEM((4, 16, 8, 128), F32),
            pltpu.VMEM((2, 128, 128), F32),
            pltpu.VMEM((3, 4, 4, 64, 128), F32),
            pltpu.VMEM((3, 4, 256, 128), F32),
            pltpu.VMEM((3, 4, 64, 128), F32),
            pltpu.VMEM((3, 4, 64, 128), F32),
            pltpu.SemaphoreType.DMA((3,)),
            pltpu.SemaphoreType.DMA((3, 4)),
            pltpu.SemaphoreType.DMA((3, 4)),
            pltpu.SemaphoreType.DMA((2,)),
            pltpu.SemaphoreType.DMA((2,)),
            pltpu.SemaphoreType.DMA((4,)),
            pltpu.SemaphoreType.DMA((4,)),
            pltpu.SemaphoreType.DMA((4, 4)),
            pltpu.SemaphoreType.DMA((4, 4)),
        ],
        compiler_params=pltpu.CompilerParams(
            collective_id=0, has_side_effects=True, vmem_limit_bytes=63 * 1024 * 1024,
        ),
    )(
        cand_blocks,
        cand_counts,
        vectors.reshape(4, 1024, 256),
        codebook.reshape(4, 4, 4, 64, 256),
    )
    return out.reshape(256, 256)


def solution(mesh):
    return jax.shard_map(
        local,
        mesh=mesh,
        in_specs=(P("dp", None), P("code", None), P("dp", "code", None), P("dp", "code")),
        out_specs=P(("code", "dp"), None),
        check_vma=False,
    )
```

```python
import functools
import math

import jax
import jax.numpy as jnp
from jax import lax
from jax.experimental import pallas as pl
from jax.experimental.pallas import tpu as pltpu
from jax.sharding import PartitionSpec as P

MESH = pl.DeviceIdType.MESH
LOG2E = 1.0 / math.log(2.0)
EPS = math.exp(-3.0)
F32 = jnp.float32
BF16 = jnp.bfloat16
F8 = jnp.float8_e5m2
NP = 8
CH = 1024 // NP
Q = CH // 4
LAG1 = 2
LAG2 = 6
LAG3 = 9
DIRECT = 1
NT = (((1,), (1,)), ((), ()))


def split(v):
    hi = v.astype(BF16)
    return hi, (v - hi.astype(F32)).astype(BF16)


def repeat8(a):
    return jnp.concatenate([a] * 8, axis=1)


def spread(v):
    return jnp.broadcast_to(v, (128, 128)).T


def wait_bytes(ref, sem):
    pltpu.make_async_copy(ref, ref, sem).wait()


def kernel(
    blocks, counts, x_hbm, c_hbm, out_ref,
    e, s, ccat, xcat, x8, bias, arep, raw0, raw1, cown,
    rg0, rg, alpha, gvec, dg, my, mz, mrep, ya, yb, yc, yd, za, zb, zc, zd, u0, u1,
    c_sem, r_send, r_recv, d_send, d_recv, m_send, m_recv, p_send, p_recv,
):
    dp = lax.axis_index("dp")
    code = lax.axis_index("code")
    z, y = dp // 4, dp % 4
    raws = (raw0, raw1)

    code_peers = [(dp, (code + d) % 8) for d in range(8)]
    dp_peers = [((dp + d) % 16, code) for d in range(16)]

    def z_peer(d):
        return (((z + d) % 4) * 4 + y, code)

    def y_peer(d):
        return (z * 4 + (y + d) % 4, code)

    def push(src, dst, send, recv, peer):
        pltpu.make_async_remote_copy(
            src_ref=src, dst_ref=dst, send_sem=send, recv_sem=recv,
            device_id=peer, device_id_type=MESH,
        ).start()

    for h in range(2):
        for p in range(NP):
            pltpu.make_async_copy(
                c_hbm.at[:, :, p, :, pl.ds(h * 128, 128)], s.at[h, :, p], c_sem.at[0]
            ).start()
    for r in range(4):
        pltpu.make_async_copy(x_hbm.at[r], e.at[7, :, pl.ds(r * 256, 256)], c_sem.at[1]).start()
    own_copy = pltpu.make_async_copy(c_hbm.at[z, y], cown, c_sem.at[2])
    own_copy.start()

    barrier = pltpu.get_barrier_semaphore()
    for d in range(1, 8):
        pl.semaphore_signal(barrier, inc=1, device_id=code_peers[d], device_id_type=MESH)
    for d in range(1, 16):
        pl.semaphore_signal(barrier, inc=1, device_id=dp_peers[d], device_id_type=MESH)

    wait_bytes(s, c_sem.at[0])

    def prepare(n, carry):
        b, p = n // NP, n % NP
        c0 = s[0, b, p].reshape(CH, 128)
        c1 = s[1, b, p].reshape(CH, 128)
        norm = jnp.sum(c0 * c0 + c1 * c1, axis=1, keepdims=True) * (-0.25 * LOG2E)
        rows = pl.ds(pl.multiple_of(p * CH, CH), CH)
        bias[b, rows, :] = jnp.broadcast_to(norm, (CH, 128))
        for h, part in enumerate((c0, c1)):
            hi, lo = split(part * (0.5 * LOG2E))
            ccat[b, rows, h * 128:(h + 1) * 128] = hi
            ccat[b, rows, 256 + h * 128:256 + (h + 1) * 128] = lo
        return carry

    lax.fori_loop(0, 4 * NP, prepare, 0)
    wait_bytes(e.at[7], c_sem.at[1])

    def score(r, iq):
        raw = raws[iq % 2]
        lanes = slice(iq * 256, (iq + 1) * 256)
        xs = e[7, lanes, pl.ds(pl.multiple_of(r * 256, 256), 256)]
        xh, xl = split(xs)
        xcat[r, lanes, 0:256] = xh
        x8[r, lanes, :] = ((xs - xh.astype(F32)) * 256.0).astype(F8)
        x8[r, iq * 256 + 1024:iq * 256 + 1280, :] = xs.astype(F8)
        rhs = jnp.concatenate([xh, xl, xh], axis=1)
        top = None
        for slot in range(2):
            b = blocks[r, 0, slot]
            ch = ccat[b, :, 0:256]
            cl = ccat[b, :, 256:512]
            lhs = jnp.concatenate([ch, ch, cl], axis=1)
            bb = bias[b]
            value = lax.dot_general(lhs, rhs, NT, preferred_element_type=F32)
            value = value + jnp.concatenate([bb, bb], axis=1)
            raw[slot * 4:slot * 4 + 4] = value.reshape(4, 256, 256)
            peak = jnp.max(value.reshape(128, 8, 256), axis=0)
            peak = jnp.max(peak, axis=0, keepdims=True)
            if slot == 0:
                top = peak
            else:
                top = jnp.where(counts[r, 0] > 1, jnp.maximum(top, peak), top)
        rg0[r, code, :, lanes] = top

    def expo(r, iq):
        raw = raws[iq % 2]
        lanes = slice(iq * 256, (iq + 1) * 256)
        top = rg0[r, code, :, lanes]
        total = jnp.zeros((8, 256), F32)
        for slot in range(2):
            shift = top if slot == 0 else jnp.where(counts[r, 0] > 1, top, 3e38)
            for k in range(0, 1024, 256):
                rows = slice(k, k + 256)
                w = jnp.exp2(raw[slot * 4 + k // 256] - shift)
                e[r * 2 + slot, rows, lanes] = w
                total = total + jnp.sum(w.reshape(32, 8, 256), axis=0)
        rg0[r, code, :, 1024 + iq * 256:1280 + iq * 256] = jnp.sum(total, axis=0, keepdims=True)

    def send_first(r):
        for d in range(1, 8):
            push(rg0.at[r, code], rg0.at[r, code], r_send.at[0, r], r_recv.at[0, r], code_peers[d])

    score(0, 0)

    def row_first(r, carry):
        for iq in range(3):
            score(r, iq + 1)
            expo(r, iq)

        @pl.when(r == 0)
        def _():
            pl.semaphore_wait(barrier, 22)

        score(r + 1, 0)
        expo(r, 3)
        send_first(r)
        return carry

    lax.fori_loop(0, 3, row_first, 0)
    for iq in range(3):
        score(3, iq + 1)
        expo(3, iq)
    expo(3, 3)
    send_first(3)

    def col_block(r):
        g = gvec[r]
        for slot in range(2):
            def chunk(n, carry):
                k = pl.ds(pl.multiple_of(n * 256, 256), 256)
                w = e[r * 2 + slot, k, :] * g
                acc = w[:, 0:128]
                for j in range(1, 8):
                    acc = acc + w[:, j * 128:(j + 1) * 128]
                s[r // 2, (r % 2) * 2 + slot, pl.ds(n * 2, 2)] = acc.reshape(2, 4, Q, 128)
                return carry

            lax.fori_loop(0, 4, chunk, 0)

    def col_first(r, carry):
        wait_bytes(rg0.at[r, pl.ds(0, 7)], r_recv.at[0, r])
        tops = [rg0[r, j, :, 0:1024] for j in range(8)]
        best = functools.reduce(jnp.maximum, tops)
        total = jnp.zeros((1, 1024), F32)
        for j in range(8):
            total = total + jnp.exp2(tops[j] - best) * rg0[r, j, :, 1024:2048]
        mine = jnp.exp2(rg0[r, code, :, 0:1024] - best)
        alpha[r] = mine
        gvec[r] = mine / total
        col_block(r)
        return carry

    def factor(it, r):
        wait_bytes(rg.at[it, r, pl.ds(0, 7)], r_recv.at[it + 1, r])
        total = rg[it, r, 0]
        for j in range(1, 8):
            total = total + rg[it, r, j]
        gvec[r] = alpha[r] / total

    def col_next(r, carry):
        factor(0, r)
        col_block(r)
        return carry

    def row_next(it):
        def body(r, carry):
            acc = jnp.zeros((8, 1024), F32)
            for slot in range(2):
                b = blocks[r, 0, slot]

                def chunk(n, acc):
                    k = pl.ds(pl.multiple_of(n * 256, 256), 256)
                    w = e[r * 2 + slot, k, :] * repeat8(arep[b, k, :])
                    return acc + jnp.sum(w.reshape(32, 8, 1024), axis=0)

                acc = lax.fori_loop(0, 4, chunk, acc)
            rg[it, r, code] = jnp.sum(acc, axis=0, keepdims=True) * alpha[r]
            for d in range(1, 8):
                push(
                    rg.at[it, r, code], rg.at[it, r, code],
                    r_send.at[it + 1, r], r_recv.at[it + 1, r], code_peers[d],
                )
            return carry

        return body

    def has_slot(r, b):
        second = (blocks[r, 0, 1] == b) & (counts[r, 0] > 1)
        slot = jnp.where(second, 1, 0)
        has = second | (blocks[r, 0, 0] == b)
        return has, slot

    def next_a(it):
        def gather(b, carry):
            for p in range(NP):
                total = jnp.zeros((4, Q, 128), F32)
                for r in range(4):
                    has, slot = has_slot(r, b)
                    total = total + jnp.where(has, s[r // 2, (r % 2) * 2 + slot, p], 0.0)
                row = jnp.sum(total.reshape(128, 128).T, axis=0, keepdims=True)
                dg[it, b, dp, p:p + 1, :] = row
            for d in range(1, 16):
                push(dg.at[it, b, dp], dg.at[it, b, dp], d_send.at[it, b], d_recv.at[it, b], dp_peers[d])
            return carry

        lax.fori_loop(0, 4, gather, 0)

        def lay(b, carry):
            wait_bytes(dg.at[it, b, pl.ds(0, 15)], d_recv.at[it, b])
            parts = [dg[it, b, j] for j in range(16)]
            while len(parts) > 1:
                parts = [parts[j] + parts[j + 1] for j in range(0, len(parts), 2)]
            a = 1.0 / (parts[0] + EPS)
            for j in range(8):
                arep[b, j * 128:(j + 1) * 128, :] = spread(a[j:j + 1, :])
            return carry

        lax.fori_loop(0, 4, lay, 0)

    lax.fori_loop(0, 4, col_first, 0)
    next_a(0)
    lax.fori_loop(0, 4, row_next(0), 0)
    lax.fori_loop(0, 4, col_next, 0)
    next_a(1)
    lax.fori_loop(0, 4, row_next(1), 0)

    def last_factor(r, carry):
        factor(1, r)
        return carry

    lax.fori_loop(0, 4, last_factor, 0)

    def part(p):
        rows = pl.ds(pl.multiple_of(p * CH, CH), CH)

        def one(r, carry):
            xh = xcat[r, :, 0:256]
            g = gvec[r]
            parts = []
            for slot in range(2):
                w = (e[r * 2 + slot, rows, :] * g) * repeat8(arep[blocks[r, 0, slot], rows, :])
                acc = w[:, 0:128]
                for j in range(1, 8):
                    acc = acc + w[:, j * 128:(j + 1) * 128]
                raw1[r * 2 + slot, 0:CH, 0:128] = acc
                hi = w.astype(BF16)
                lo = w - hi.astype(F32)
                parts.append((hi, jnp.concatenate([(w * 2.0**15).astype(F8), (lo * 2.0**23).astype(F8)], axis=1)))
            eh = jnp.concatenate([hi for hi, lo in parts], axis=0)
            el = jnp.concatenate([lo for hi, lo in parts], axis=0)
            value = jnp.dot(eh, xh, preferred_element_type=F32)
            value = value + jnp.dot(el, x8[r], preferred_element_type=F32) * 2.0**-23
            for slot in range(2):
                raw0[r * 2 + slot, 0:CH, :] = value[slot * CH:(slot + 1) * CH]
            return carry

        lax.fori_loop(0, 4, one, 0)
        for b in range(4):
            total = jnp.zeros((CH, 256), F32)
            mass = jnp.zeros((CH, 128), F32)
            for r in range(4):
                has, slot = has_slot(r, b)
                total = total + jnp.where(has, raw0[r * 2 + slot, 0:CH, :], 0.0)
                mass = mass + jnp.where(has, raw1[r * 2 + slot, 0:CH, 0:128], 0.0)
            s[0, b, p] = total[:, 0:128].reshape(4, Q, 128)
            s[1, b, p] = total[:, 128:256].reshape(4, Q, 128)
            my[p // 2, y, pl.ds((p % 2) * 4 + b, 1), :] = jnp.sum(mass.T, axis=0, keepdims=True)

    y_next, y_last, y_far = (y + 1) % 4, (y + 3) % 4, (y + 2) % 4
    z_next, z_last, z_far = (z + 1) % 4, (z + 3) % 4, (z + 2) % 4
    to_y_next, to_y_last = y_peer(1), y_peer(3)
    to_z_next, to_z_last = z_peer(1), z_peer(3)

    def far_parts(p, peers):
        push(s.at[0, pl.ds(0, 2), p, y_far], ya.at[p], p_send.at[0, p], p_recv.at[0, p], peers[0])
        push(s.at[1, z_far, p, pl.ds(0, 2)], za.at[p], p_send.at[2, p], p_recv.at[2, p], peers[1])
        push(s.at[0, pl.ds(2, 2), p, y_far], yb.at[p], p_send.at[1, p], p_recv.at[1, p], peers[2])
        push(s.at[1, z_far, p, pl.ds(2, 2)], zb.at[p], p_send.at[3, p], p_recv.at[3, p], peers[3])

    def next_y(p):
        push(s.at[0, :, p, y_next], yc.at[p], p_send.at[4, p], p_recv.at[4, p], to_y_next)

    def next_z(p):
        push(s.at[1, z_next, p], zc.at[p], p_send.at[6, p], p_recv.at[6, p], to_z_next)

    def last_y(p):
        push(s.at[0, :, p, y_last], yd.at[p], p_send.at[5, p], p_recv.at[5, p], to_y_last)

    def last_z(p):
        push(s.at[1, z_last, p], zd.at[p], p_send.at[7, p], p_recv.at[7, p], to_z_last)

    def step_one(p):
        @pl.when(p < NP - DIRECT)
        def _():
            far_parts(p, (to_y_next, to_z_next, to_y_last, to_z_last))

        @pl.when(p >= NP - DIRECT)
        def _():
            far_parts(p, (y_peer(2), z_peer(2), y_peer(2), z_peer(2)))
            next_y(p)
            next_z(p)
            last_y(p)
            last_z(p)

        @pl.when(p % 2 == 1)
        def _():
            for d in range(1, 4):
                push(my.at[p // 2, y], my.at[p // 2, y], m_send.at[0, p // 2], m_recv.at[0, p // 2], y_peer(d))

    def step_two(p):
        wait_bytes(ya.at[p], p_recv.at[0, p])
        s[0, 0:2, p, y_next] = s[0, 0:2, p, y_next] + ya[p]
        next_y(p)
        wait_bytes(za.at[p], p_recv.at[2, p])
        s[1, z_next, p, 0:2] = s[1, z_next, p, 0:2] + za[p]
        next_z(p)
        wait_bytes(yb.at[p], p_recv.at[1, p])
        s[0, 2:4, p, y_last] = s[0, 2:4, p, y_last] + yb[p]
        last_y(p)
        wait_bytes(zb.at[p], p_recv.at[3, p])
        s[1, z_last, p, 2:4] = s[1, z_last, p, 2:4] + zb[p]
        last_z(p)

    def step_three(p):
        wait_bytes(yc.at[p], p_recv.at[4, p])
        wait_bytes(yd.at[p], p_recv.at[5, p])

        @pl.when(p >= NP - DIRECT)
        def _():
            for n, ref in enumerate((ya, yb, za, zb)):
                wait_bytes(ref.at[p], p_recv.at[n, p])
            s[0, 0:2, p, y] = s[0, 0:2, p, y] + ya[p]
            s[0, 2:4, p, y] = s[0, 2:4, p, y] + yb[p]
            s[1, z, p, 0:2] = s[1, z, p, 0:2] + za[p]
            s[1, z, p, 2:4] = s[1, z, p, 2:4] + zb[p]

        s[0, :, p, y] = (s[0, :, p, y] + yc[p]) + yd[p]
        for d in range(1, 4):
            push(s.at[0, (z + d) % 4, p, y], u0.at[d - 1, p], p_send.at[8, p], p_recv.at[8, p], z_peer(d))
        wait_bytes(zc.at[p], p_recv.at[6, p])
        wait_bytes(zd.at[p], p_recv.at[7, p])
        s[1, z, p] = (s[1, z, p] + zc[p]) + zd[p]
        for d in range(1, 4):
            push(s.at[1, z, p, (y + d) % 4], u1.at[d - 1, p], p_send.at[9, p], p_recv.at[9, p], y_peer(d))

        @pl.when(p % 2 == 1)
        def _():
            n = p // 2
            wait_bytes(my.at[n, pl.ds(0, 3)], m_recv.at[0, n])
            mz[n, z] = (my[n, 0] + my[n, 1]) + (my[n, 2] + my[n, 3])
            for d in range(1, 4):
                push(mz.at[n, z], mz.at[n, z], m_send.at[1, n], m_recv.at[1, n], z_peer(d))

    own_copy.wait()

    def finish(p):
        @pl.when(p % 2 == 0)
        def _():
            n = p // 2
            wait_bytes(mz.at[n, pl.ds(0, 3)], m_recv.at[1, n])
            mass = (mz[n, 0] + mz[n, 1]) + (mz[n, 2] + mz[n, 3])
            mrep[1, 0:8, :] = mass

        mrep[0] = spread(mrep[1, pl.ds((p % 2) * 4 + z, 1), :])
        slack = EPS * arep[z, pl.ds(pl.multiple_of(p * CH + y * Q, Q), Q), :]
        a = 1.0 / (mrep[0, pl.ds(pl.multiple_of(y * Q, Q), Q), :] + slack)
        wait_bytes(u0.at[:, p], p_recv.at[8, p])
        wait_bytes(u1.at[:, p], p_recv.at[9, p])
        f0 = (s[0, z, p, y] + u0[0, p]) + (u0[1, p] + u0[2, p])
        f1 = (s[1, z, p, y] + u1[0, p]) + (u1[1, p] + u1[2, p])
        out_ref[p, :, 0:128] = (f0 + slack * cown[p, :, 0:128]) * a
        out_ref[p, :, 128:256] = (f1 + slack * cown[p, :, 128:256]) * a

    def final(n, carry):
        @pl.when(n < NP)
        def _():
            part(n)
            step_one(n)

        @pl.when((n >= LAG1) & (n < NP - DIRECT + LAG1))
        def _():
            step_two(n - LAG1)

        @pl.when((n >= LAG2) & (n < NP + LAG2))
        def _():
            step_three(n - LAG2)

        @pl.when(n >= LAG3)
        def _():
            finish(n - LAG3)

        return carry

    lax.fori_loop(0, NP + LAG3, final, 0)

    def drain_rows(r, carry):
        wait_bytes(rg0.at[r, pl.ds(0, 7)], r_send.at[0, r])
        wait_bytes(rg.at[0, r, pl.ds(0, 7)], r_send.at[1, r])
        wait_bytes(rg.at[1, r, pl.ds(0, 7)], r_send.at[2, r])
        wait_bytes(my.at[r, pl.ds(0, 3)], m_send.at[0, r])
        wait_bytes(mz.at[r, pl.ds(0, 3)], m_send.at[1, r])
        return carry

    lax.fori_loop(0, 4, drain_rows, 0)

    def drain_parts(p, carry):
        for n, ref in enumerate((ya, yb, za, zb, yc, yd, zc, zd)):
            wait_bytes(ref.at[p], p_send.at[n, p])
        wait_bytes(u0.at[:, p], p_send.at[8, p])
        wait_bytes(u1.at[:, p], p_send.at[9, p])
        return carry

    lax.fori_loop(0, NP, drain_parts, 0)
    for it in range(2):
        for b in range(4):
            wait_bytes(dg.at[it, b, pl.ds(0, 15)], d_send.at[it, b])


def local(vectors, codebook, cand_blocks, cand_counts):
    smem = pl.BlockSpec(memory_space=pltpu.SMEM)
    hbm = pl.BlockSpec(memory_space=pl.ANY)
    out = pl.pallas_call(
        kernel,
        out_shape=jax.ShapeDtypeStruct((NP, Q, 256), F32),
        in_specs=[smem, smem, hbm, hbm],
        out_specs=pl.BlockSpec(memory_space=pltpu.VMEM),
        scratch_shapes=[
            pltpu.VMEM((8, 1024, 1024), F32),
            pltpu.VMEM((2, 4, NP, 4, Q, 128), F32),
            pltpu.VMEM((4, 1024, 512), BF16),
            pltpu.VMEM((4, 1024, 256), BF16),
            pltpu.VMEM((4, 2048, 256), F8),
            pltpu.VMEM((4, 1024, 128), F32),
            pltpu.VMEM((4, 1024, 128), F32),
            pltpu.VMEM((8, 256, 256), F32),
            pltpu.VMEM((8, 256, 256), F32),
            pltpu.VMEM((NP, Q, 256), F32),
            pltpu.VMEM((4, 8, 1, 2048), F32),
            pltpu.VMEM((2, 4, 8, 1, 1024), F32),
            pltpu.VMEM((4, 1, 1024), F32),
            pltpu.VMEM((4, 1, 1024), F32),
            pltpu.VMEM((2, 4, 16, 8, 128), F32),
            pltpu.VMEM((4, 4, 8, 128), F32),
            pltpu.VMEM((4, 4, 8, 128), F32),
            pltpu.VMEM((2, 128, 128), F32),
            pltpu.VMEM((NP, 2, Q, 128), F32),
            pltpu.VMEM((NP, 2, Q, 128), F32),
            pltpu.VMEM((NP, 4, Q, 128), F32),
            pltpu.VMEM((NP, 4, Q, 128), F32),
            pltpu.VMEM((NP, 2, Q, 128), F32),
            pltpu.VMEM((NP, 2, Q, 128), F32),
            pltpu.VMEM((NP, 4, Q, 128), F32),
            pltpu.VMEM((NP, 4, Q, 128), F32),
            pltpu.VMEM((3, NP, Q, 128), F32),
            pltpu.VMEM((3, NP, Q, 128), F32),
            pltpu.SemaphoreType.DMA((3,)),
            pltpu.SemaphoreType.DMA((3, 4)),
            pltpu.SemaphoreType.DMA((3, 4)),
            pltpu.SemaphoreType.DMA((2, 4)),
            pltpu.SemaphoreType.DMA((2, 4)),
            pltpu.SemaphoreType.DMA((2, 4)),
            pltpu.SemaphoreType.DMA((2, 4)),
            pltpu.SemaphoreType.DMA((10, NP)),
            pltpu.SemaphoreType.DMA((10, NP)),
        ],
        compiler_params=pltpu.CompilerParams(
            collective_id=0, has_side_effects=True, vmem_limit_bytes=63 * 1024 * 1024,
        ),
    )(
        cand_blocks,
        cand_counts,
        vectors.reshape(4, 1024, 256),
        codebook.reshape(4, 4, NP, Q, 256),
    )
    return out.reshape(256, 256)


def solution(mesh):
    return jax.shard_map(
        local,
        mesh=mesh,
        in_specs=(P("dp", None), P("code", None), P("dp", "code", None), P("dp", "code")),
        out_specs=P(("code", "dp"), None),
        check_vma=False,
    )
```

```python
import functools
import math

import jax
import jax.numpy as jnp
from jax import lax
from jax.experimental import pallas as pl
from jax.experimental.pallas import tpu as pltpu
from jax.sharding import PartitionSpec as P

MESH = pl.DeviceIdType.MESH
LOG2E = 1.0 / math.log(2.0)
EPS = math.exp(-3.0)
F32 = jnp.float32
BF16 = jnp.bfloat16
F8 = jnp.float8_e5m2
NP = 8
CH = 1024 // NP
Q = CH // 4
LAG1 = 2
LAG2 = 6
LAG3 = 9
DIRECT = 1
NT = (((1,), (1,)), ((), ()))


def split(v):
    hi = v.astype(BF16)
    return hi, (v - hi.astype(F32)).astype(BF16)


def repeat8(a):
    return jnp.concatenate([a] * 8, axis=1)


def spread(v):
    return jnp.broadcast_to(v, (128, 128)).T


def wait_bytes(ref, sem):
    pltpu.make_async_copy(ref, ref, sem).wait()


def kernel(
    blocks, counts, x_hbm, c_hbm, out_ref,
    e, s, ccat, xcat, x8, bias, arep, raw0, raw1, cown,
    rg0, rg, alpha, gvec, dg, my, mz, mrep, ya, yb, yc, yd, za, zb, zc, zd, u0, u1,
    c_sem, r_send, r_recv, d_send, d_recv, m_send, m_recv, p_send, p_recv,
):
    dp = lax.axis_index("dp")
    code = lax.axis_index("code")
    z, y = dp // 4, dp % 4
    raws = (raw0, raw1)

    code_peers = [(dp, (code + d) % 8) for d in range(8)]
    steps = [(a, b) for a in range(4) for b in range(4) if a or b]
    steps.sort(key=lambda s: -(min(s[0], 4 - s[0]) + min(s[1], 4 - s[1])))
    dp_peers = [(((z + a) % 4) * 4 + (y + b) % 4, code) for a, b in steps]

    def z_peer(d):
        return (((z + d) % 4) * 4 + y, code)

    def y_peer(d):
        return (z * 4 + (y + d) % 4, code)

    def push(src, dst, send, recv, peer):
        pltpu.make_async_remote_copy(
            src_ref=src, dst_ref=dst, send_sem=send, recv_sem=recv,
            device_id=peer, device_id_type=MESH,
        ).start()

    for h in range(2):
        for p in range(NP):
            pltpu.make_async_copy(
                c_hbm.at[:, :, p, :, pl.ds(h * 128, 128)], s.at[h, :, p], c_sem.at[0]
            ).start()
    for r in range(4):
        pltpu.make_async_copy(x_hbm.at[r], e.at[7, :, pl.ds(r * 256, 256)], c_sem.at[1]).start()
    own_copy = pltpu.make_async_copy(c_hbm.at[z, y], cown, c_sem.at[2])
    own_copy.start()

    barrier = pltpu.get_barrier_semaphore()
    for d in (4, 3, 5, 2, 6, 1, 7):
        pl.semaphore_signal(barrier, inc=1, device_id=code_peers[d], device_id_type=MESH)
    for d in range(15):
        pl.semaphore_signal(barrier, inc=1, device_id=dp_peers[d], device_id_type=MESH)

    wait_bytes(s, c_sem.at[0])

    def prepare(n, carry):
        b, p = n // 2, n % 2
        half = pl.ds(p * (NP // 2), NP // 2)
        c0 = s[0, b, half].reshape(512, 128)
        c1 = s[1, b, half].reshape(512, 128)
        norm = jnp.sum(c0 * c0 + c1 * c1, axis=1, keepdims=True) * (-0.25 * LOG2E)
        rows = pl.ds(pl.multiple_of(p * 512, 512), 512)
        bias[b, rows, :] = jnp.broadcast_to(norm, (512, 128))
        for h, part in enumerate((c0, c1)):
            hi, lo = split(part * (0.5 * LOG2E))
            ccat[b, rows, h * 128:(h + 1) * 128] = hi
            ccat[b, rows, 256 + h * 128:256 + (h + 1) * 128] = lo
        return carry

    lax.fori_loop(0, 8, prepare, 0)
    wait_bytes(e.at[7], c_sem.at[1])

    def score(r, iq):
        raw = raws[iq % 2]
        lanes = slice(iq * 256, (iq + 1) * 256)
        xs = e[7, lanes, pl.ds(pl.multiple_of(r * 256, 256), 256)]
        xh, xl = split(xs)
        xcat[r, lanes, 0:256] = xh
        x8[r, lanes, :] = ((xs - xh.astype(F32)) * 256.0).astype(F8)
        x8[r, iq * 256 + 1024:iq * 256 + 1280, :] = xs.astype(F8)
        rhs = jnp.concatenate([xh, xl, xh], axis=1)
        top = None
        for slot in range(2):
            b = blocks[r, 0, slot]
            ch = ccat[b, :, 0:256]
            cl = ccat[b, :, 256:512]
            lhs = jnp.concatenate([ch, ch, cl], axis=1)
            bb = bias[b]
            value = lax.dot_general(lhs, rhs, NT, preferred_element_type=F32)
            value = value + jnp.concatenate([bb, bb], axis=1)
            raw[slot * 4:slot * 4 + 4] = value.reshape(4, 256, 256)
            peak = jnp.max(value.reshape(128, 8, 256), axis=0)
            peak = jnp.max(peak, axis=0, keepdims=True)
            if slot == 0:
                top = peak
            else:
                top = jnp.where(counts[r, 0] > 1, jnp.maximum(top, peak), top)
        rg0[r, code, :, lanes] = top

    def expo(r, iq):
        raw = raws[iq % 2]
        lanes = slice(iq * 256, (iq + 1) * 256)
        top = rg0[r, code, :, lanes]
        total = jnp.zeros((8, 256), F32)
        for slot in range(2):
            shift = top if slot == 0 else jnp.where(counts[r, 0] > 1, top, 3e38)
            for k in range(0, 1024, 256):
                rows = slice(k, k + 256)
                w = jnp.exp2(raw[slot * 4 + k // 256] - shift)
                e[r * 2 + slot, rows, lanes] = w
                total = total + jnp.sum(w.reshape(32, 8, 256), axis=0)
        rg0[r, code, :, 1024 + iq * 256:1280 + iq * 256] = jnp.sum(total, axis=0, keepdims=True)

    def send_first(r):
        for d in (4, 3, 5, 2, 6, 1, 7):
            push(rg0.at[r, code], rg0.at[r, code], r_send.at[0, r], r_recv.at[0, r], code_peers[d])

    score(0, 0)

    def row_first(r, carry):
        for iq in range(3):
            score(r, iq + 1)
            expo(r, iq)

        @pl.when(r == 0)
        def _():
            pl.semaphore_wait(barrier, 22)

        score(r + 1, 0)
        expo(r, 3)
        send_first(r)
        return carry

    lax.fori_loop(0, 3, row_first, 0)
    for iq in range(3):
        score(3, iq + 1)
        expo(3, iq)
    expo(3, 3)
    send_first(3)

    def col_block(r):
        g = gvec[r]
        for slot in range(2):
            def chunk(n, carry):
                k = pl.ds(pl.multiple_of(n * 256, 256), 256)
                w = e[r * 2 + slot, k, :] * g
                acc = w[:, 0:128]
                for j in range(1, 8):
                    acc = acc + w[:, j * 128:(j + 1) * 128]
                s[r // 2, (r % 2) * 2 + slot, pl.ds(n * 2, 2)] = acc.reshape(2, 4, Q, 128)
                return carry

            lax.fori_loop(0, 4, chunk, 0)

    def col_first(r, carry):
        wait_bytes(rg0.at[r, pl.ds(0, 7)], r_recv.at[0, r])
        tops = [rg0[r, j, :, 0:1024] for j in range(8)]
        best = functools.reduce(jnp.maximum, tops)
        total = jnp.zeros((1, 1024), F32)
        for j in range(8):
            total = total + jnp.exp2(tops[j] - best) * rg0[r, j, :, 1024:2048]
        mine = jnp.exp2(rg0[r, code, :, 0:1024] - best)
        alpha[r] = mine
        gvec[r] = mine / total
        col_block(r)
        return carry

    def factor(it, r):
        wait_bytes(rg.at[it, r, pl.ds(0, 7)], r_recv.at[it + 1, r])
        total = rg[it, r, 0]
        for j in range(1, 8):
            total = total + rg[it, r, j]
        gvec[r] = alpha[r] / total

    def col_next(r, carry):
        factor(0, r)
        col_block(r)
        return carry

    def row_next(it):
        def body(r, carry):
            acc = jnp.zeros((8, 1024), F32)
            for slot in range(2):
                b = blocks[r, 0, slot]

                def chunk(n, acc):
                    k = pl.ds(pl.multiple_of(n * 256, 256), 256)
                    w = e[r * 2 + slot, k, :] * repeat8(arep[b, k, :])
                    return acc + jnp.sum(w.reshape(32, 8, 1024), axis=0)

                acc = lax.fori_loop(0, 4, chunk, acc)
            rg[it, r, code] = jnp.sum(acc, axis=0, keepdims=True) * alpha[r]
            for d in (4, 3, 5, 2, 6, 1, 7):
                push(
                    rg.at[it, r, code], rg.at[it, r, code],
                    r_send.at[it + 1, r], r_recv.at[it + 1, r], code_peers[d],
                )
            return carry

        return body

    def has_slot(r, b):
        second = (blocks[r, 0, 1] == b) & (counts[r, 0] > 1)
        slot = jnp.where(second, 1, 0)
        has = second | (blocks[r, 0, 0] == b)
        return has, slot

    def next_a(it):
        def gather(b, carry):
            for p in range(NP):
                total = jnp.zeros((4, Q, 128), F32)
                for r in range(4):
                    has, slot = has_slot(r, b)
                    total = total + jnp.where(has, s[r // 2, (r % 2) * 2 + slot, p], 0.0)
                row = jnp.sum(total.reshape(128, 128).T, axis=0, keepdims=True)
                dg[it, b, dp, p:p + 1, :] = row
            for d in range(15):
                push(dg.at[it, b, dp], dg.at[it, b, dp], d_send.at[it, b], d_recv.at[it, b], dp_peers[d])
            return carry

        lax.fori_loop(0, 4, gather, 0)

        def lay(b, carry):
            wait_bytes(dg.at[it, b, pl.ds(0, 15)], d_recv.at[it, b])
            parts = [dg[it, b, j] for j in range(16)]
            while len(parts) > 1:
                parts = [parts[j] + parts[j + 1] for j in range(0, len(parts), 2)]
            a = 1.0 / (parts[0] + EPS)
            for j in range(8):
                arep[b, j * 128:(j + 1) * 128, :] = spread(a[j:j + 1, :])
            return carry

        lax.fori_loop(0, 4, lay, 0)

    lax.fori_loop(0, 4, col_first, 0)
    next_a(0)
    lax.fori_loop(0, 4, row_next(0), 0)
    lax.fori_loop(0, 4, col_next, 0)
    next_a(1)
    lax.fori_loop(0, 4, row_next(1), 0)

    def last_factor(r, carry):
        factor(1, r)
        return carry

    lax.fori_loop(0, 4, last_factor, 0)

    def part(p):
        rows = pl.ds(pl.multiple_of(p * CH, CH), CH)

        def one(r, carry):
            xh = xcat[r, :, 0:256]
            g = gvec[r]
            parts = []
            for slot in range(2):
                w = (e[r * 2 + slot, rows, :] * g) * repeat8(arep[blocks[r, 0, slot], rows, :])
                acc = w[:, 0:128]
                for j in range(1, 8):
                    acc = acc + w[:, j * 128:(j + 1) * 128]
                raw1[r * 2 + slot, 0:CH, 0:128] = acc
                hi = w.astype(BF16)
                lo = w - hi.astype(F32)
                parts.append((hi, jnp.concatenate([(w * 2.0**15).astype(F8), (lo * 2.0**23).astype(F8)], axis=1)))
            eh = jnp.concatenate([hi for hi, lo in parts], axis=0)
            el = jnp.concatenate([lo for hi, lo in parts], axis=0)
            value = jnp.dot(eh, xh, preferred_element_type=F32)
            value = value + jnp.dot(el, x8[r], preferred_element_type=F32) * 2.0**-23
            for slot in range(2):
                raw0[r * 2 + slot, 0:CH, :] = value[slot * CH:(slot + 1) * CH]
            return carry

        lax.fori_loop(0, 4, one, 0, unroll=2)
        for b in range(4):
            total = jnp.zeros((CH, 256), F32)
            mass = jnp.zeros((CH, 128), F32)
            for r in range(4):
                has, slot = has_slot(r, b)
                total = total + jnp.where(has, raw0[r * 2 + slot, 0:CH, :], 0.0)
                mass = mass + jnp.where(has, raw1[r * 2 + slot, 0:CH, 0:128], 0.0)
            s[0, b, p] = total[:, 0:128].reshape(4, Q, 128)
            s[1, b, p] = total[:, 128:256].reshape(4, Q, 128)
            my[p // 2, y, pl.ds((p % 2) * 4 + b, 1), :] = jnp.sum(mass.T, axis=0, keepdims=True)

    y_next, y_last, y_far = (y + 1) % 4, (y + 3) % 4, (y + 2) % 4
    z_next, z_last, z_far = (z + 1) % 4, (z + 3) % 4, (z + 2) % 4
    to_y_next, to_y_last = y_peer(1), y_peer(3)
    to_z_next, to_z_last = z_peer(1), z_peer(3)

    def far_parts(p, peers):
        push(s.at[0, pl.ds(0, 2), p, y_far], ya.at[p], p_send.at[0, p], p_recv.at[0, p], peers[0])
        push(s.at[1, z_far, p, pl.ds(0, 2)], za.at[p], p_send.at[2, p], p_recv.at[2, p], peers[1])
        push(s.at[0, pl.ds(2, 2), p, y_far], yb.at[p], p_send.at[1, p], p_recv.at[1, p], peers[2])
        push(s.at[1, z_far, p, pl.ds(2, 2)], zb.at[p], p_send.at[3, p], p_recv.at[3, p], peers[3])

    def next_y(p):
        push(s.at[0, :, p, y_next], yc.at[p], p_send.at[4, p], p_recv.at[4, p], to_y_next)

    def next_z(p):
        push(s.at[1, z_next, p], zc.at[p], p_send.at[6, p], p_recv.at[6, p], to_z_next)

    def last_y(p):
        push(s.at[0, :, p, y_last], yd.at[p], p_send.at[5, p], p_recv.at[5, p], to_y_last)

    def last_z(p):
        push(s.at[1, z_last, p], zd.at[p], p_send.at[7, p], p_recv.at[7, p], to_z_last)

    def step_one(p):
        @pl.when(p < NP - DIRECT)
        def _():
            far_parts(p, (to_y_next, to_z_next, to_y_last, to_z_last))

        @pl.when(p >= NP - DIRECT)
        def _():
            far_parts(p, (y_peer(2), z_peer(2), y_peer(2), z_peer(2)))
            next_y(p)
            next_z(p)
            last_y(p)
            last_z(p)

        @pl.when(p % 2 == 1)
        def _():
            for d in range(1, 4):
                push(my.at[p // 2, y], my.at[p // 2, y], m_send.at[0, p // 2], m_recv.at[0, p // 2], y_peer(d))

    def step_two(p):
        wait_bytes(ya.at[p], p_recv.at[0, p])
        s[0, 0:2, p, y_next] = s[0, 0:2, p, y_next] + ya[p]
        next_y(p)
        wait_bytes(za.at[p], p_recv.at[2, p])
        s[1, z_next, p, 0:2] = s[1, z_next, p, 0:2] + za[p]
        next_z(p)
        wait_bytes(yb.at[p], p_recv.at[1, p])
        s[0, 2:4, p, y_last] = s[0, 2:4, p, y_last] + yb[p]
        last_y(p)
        wait_bytes(zb.at[p], p_recv.at[3, p])
        s[1, z_last, p, 2:4] = s[1, z_last, p, 2:4] + zb[p]
        last_z(p)

    def step_three(p):
        wait_bytes(yc.at[p], p_recv.at[4, p])
        wait_bytes(yd.at[p], p_recv.at[5, p])

        @pl.when(p >= NP - DIRECT)
        def _():
            for n, ref in enumerate((ya, yb, za, zb)):
                wait_bytes(ref.at[p], p_recv.at[n, p])
            s[0, 0:2, p, y] = s[0, 0:2, p, y] + ya[p]
            s[0, 2:4, p, y] = s[0, 2:4, p, y] + yb[p]
            s[1, z, p, 0:2] = s[1, z, p, 0:2] + za[p]
            s[1, z, p, 2:4] = s[1, z, p, 2:4] + zb[p]

        s[0, :, p, y] = (s[0, :, p, y] + yc[p]) + yd[p]
        for d in range(1, 4):
            push(s.at[0, (z + d) % 4, p, y], u0.at[d - 1, p], p_send.at[8, p], p_recv.at[8, p], z_peer(d))
        wait_bytes(zc.at[p], p_recv.at[6, p])
        wait_bytes(zd.at[p], p_recv.at[7, p])
        s[1, z, p] = (s[1, z, p] + zc[p]) + zd[p]
        for d in range(1, 4):
            push(s.at[1, z, p, (y + d) % 4], u1.at[d - 1, p], p_send.at[9, p], p_recv.at[9, p], y_peer(d))

        @pl.when(p % 2 == 1)
        def _():
            n = p // 2
            wait_bytes(my.at[n, pl.ds(0, 3)], m_recv.at[0, n])
            mz[n, z] = (my[n, 0] + my[n, 1]) + (my[n, 2] + my[n, 3])
            for d in range(1, 4):
                push(mz.at[n, z], mz.at[n, z], m_send.at[1, n], m_recv.at[1, n], z_peer(d))

    own_copy.wait()

    def finish(p):
        @pl.when(p % 2 == 0)
        def _():
            n = p // 2
            wait_bytes(mz.at[n, pl.ds(0, 3)], m_recv.at[1, n])
            mass = (mz[n, 0] + mz[n, 1]) + (mz[n, 2] + mz[n, 3])
            mrep[1, 0:8, :] = mass

        mrep[0] = spread(mrep[1, pl.ds((p % 2) * 4 + z, 1), :])
        slack = EPS * arep[z, pl.ds(pl.multiple_of(p * CH + y * Q, Q), Q), :]
        a = 1.0 / (mrep[0, pl.ds(pl.multiple_of(y * Q, Q), Q), :] + slack)
        wait_bytes(u0.at[:, p], p_recv.at[8, p])
        wait_bytes(u1.at[:, p], p_recv.at[9, p])
        f0 = (s[0, z, p, y] + u0[0, p]) + (u0[1, p] + u0[2, p])
        f1 = (s[1, z, p, y] + u1[0, p]) + (u1[1, p] + u1[2, p])
        out_ref[p, :, 0:128] = (f0 + slack * cown[p, :, 0:128]) * a
        out_ref[p, :, 128:256] = (f1 + slack * cown[p, :, 128:256]) * a

    def final(n, carry):
        @pl.when(n < NP)
        def _():
            part(n)
            step_one(n)

        @pl.when((n >= LAG1) & (n < NP - DIRECT + LAG1))
        def _():
            step_two(n - LAG1)

        @pl.when((n >= LAG2) & (n < NP + LAG2))
        def _():
            step_three(n - LAG2)

        @pl.when(n >= LAG3)
        def _():
            finish(n - LAG3)

        return carry

    lax.fori_loop(0, NP + LAG3, final, 0)

    def drain_rows(r, carry):
        wait_bytes(rg0.at[r, pl.ds(0, 7)], r_send.at[0, r])
        wait_bytes(rg.at[0, r, pl.ds(0, 7)], r_send.at[1, r])
        wait_bytes(rg.at[1, r, pl.ds(0, 7)], r_send.at[2, r])
        wait_bytes(my.at[r, pl.ds(0, 3)], m_send.at[0, r])
        wait_bytes(mz.at[r, pl.ds(0, 3)], m_send.at[1, r])
        return carry

    lax.fori_loop(0, 4, drain_rows, 0)

    def drain_parts(p, carry):
        for n, ref in enumerate((ya, yb, za, zb, yc, yd, zc, zd)):
            wait_bytes(ref.at[p], p_send.at[n, p])
        wait_bytes(u0.at[:, p], p_send.at[8, p])
        wait_bytes(u1.at[:, p], p_send.at[9, p])
        return carry

    lax.fori_loop(0, NP, drain_parts, 0)
    for it in range(2):
        for b in range(4):
            wait_bytes(dg.at[it, b, pl.ds(0, 15)], d_send.at[it, b])


def local(vectors, codebook, cand_blocks, cand_counts):
    smem = pl.BlockSpec(memory_space=pltpu.SMEM)
    hbm = pl.BlockSpec(memory_space=pl.ANY)
    out = pl.pallas_call(
        kernel,
        out_shape=jax.ShapeDtypeStruct((NP, Q, 256), F32),
        in_specs=[smem, smem, hbm, hbm],
        out_specs=pl.BlockSpec(memory_space=pltpu.VMEM),
        scratch_shapes=[
            pltpu.VMEM((8, 1024, 1024), F32),
            pltpu.VMEM((2, 4, NP, 4, Q, 128), F32),
            pltpu.VMEM((4, 1024, 512), BF16),
            pltpu.VMEM((4, 1024, 256), BF16),
            pltpu.VMEM((4, 2048, 256), F8),
            pltpu.VMEM((4, 1024, 128), F32),
            pltpu.VMEM((4, 1024, 128), F32),
            pltpu.VMEM((8, 256, 256), F32),
            pltpu.VMEM((8, 256, 256), F32),
            pltpu.VMEM((NP, Q, 256), F32),
            pltpu.VMEM((4, 8, 1, 2048), F32),
            pltpu.VMEM((2, 4, 8, 1, 1024), F32),
            pltpu.VMEM((4, 1, 1024), F32),
            pltpu.VMEM((4, 1, 1024), F32),
            pltpu.VMEM((2, 4, 16, 8, 128), F32),
            pltpu.VMEM((4, 4, 8, 128), F32),
            pltpu.VMEM((4, 4, 8, 128), F32),
            pltpu.VMEM((2, 128, 128), F32),
            pltpu.VMEM((NP, 2, Q, 128), F32),
            pltpu.VMEM((NP, 2, Q, 128), F32),
            pltpu.VMEM((NP, 4, Q, 128), F32),
            pltpu.VMEM((NP, 4, Q, 128), F32),
            pltpu.VMEM((NP, 2, Q, 128), F32),
            pltpu.VMEM((NP, 2, Q, 128), F32),
            pltpu.VMEM((NP, 4, Q, 128), F32),
            pltpu.VMEM((NP, 4, Q, 128), F32),
            pltpu.VMEM((3, NP, Q, 128), F32),
            pltpu.VMEM((3, NP, Q, 128), F32),
            pltpu.SemaphoreType.DMA((3,)),
            pltpu.SemaphoreType.DMA((3, 4)),
            pltpu.SemaphoreType.DMA((3, 4)),
            pltpu.SemaphoreType.DMA((2, 4)),
            pltpu.SemaphoreType.DMA((2, 4)),
            pltpu.SemaphoreType.DMA((2, 4)),
            pltpu.SemaphoreType.DMA((2, 4)),
            pltpu.SemaphoreType.DMA((10, NP)),
            pltpu.SemaphoreType.DMA((10, NP)),
        ],
        compiler_params=pltpu.CompilerParams(
            collective_id=0, has_side_effects=True, vmem_limit_bytes=63 * 1024 * 1024,
        ),
    )(
        cand_blocks,
        cand_counts,
        vectors.reshape(4, 1024, 256),
        codebook.reshape(4, 4, NP, Q, 256),
    )
    return out.reshape(256, 256)


def solution(mesh):
    return jax.shard_map(
        local,
        mesh=mesh,
        in_specs=(P("dp", None), P("code", None), P("dp", "code", None), P("dp", "code")),
        out_specs=P(("code", "dp"), None),
        check_vma=False,
    )
```

```python
import functools
import math

import jax
import jax.numpy as jnp
from jax import lax
from jax.experimental import pallas as pl
from jax.experimental.pallas import tpu as pltpu
from jax.sharding import PartitionSpec as P

MESH = pl.DeviceIdType.MESH
LOG2E = 1.0 / math.log(2.0)
EPS = math.exp(-3.0)
F32 = jnp.float32
BF16 = jnp.bfloat16
F8 = jnp.float8_e5m2
NP = 8
CH = 1024 // NP
Q = CH // 4
LAG1 = 2
LAG2 = 6
LAG3 = 9
DIRECT = 1
NT = (((1,), (1,)), ((), ()))


def split(v):
    hi = v.astype(BF16)
    return hi, (v - hi.astype(F32)).astype(BF16)


def repeat8(a):
    return jnp.concatenate([a] * 8, axis=1)


def spread(v):
    return jnp.broadcast_to(v, (128, 128)).T


def wait_bytes(ref, sem):
    pltpu.make_async_copy(ref, ref, sem).wait()


def kernel(
    blocks, counts, x_hbm, c_hbm, out_ref,
    e, s, ccat, xcat, x8, bias, arep, raw0, raw1, cown,
    rg0, rg, alpha, gvec, dg, my, mz, mrep, ya, yb, yc, yd, za, zb, zc, zd, u0, u1,
    c_sem, r_send, r_recv, d_send, d_recv, m_send, m_recv, p_send, p_recv,
):
    dp = lax.axis_index("dp")
    code = lax.axis_index("code")
    z, y = dp // 4, dp % 4
    raws = (raw0, raw1)

    code_peers = [(dp, (code + d) % 8) for d in range(8)]
    steps = [(a, b) for a in range(4) for b in range(4) if a or b]
    steps.sort(key=lambda s: -(min(s[0], 4 - s[0]) + min(s[1], 4 - s[1])))
    dp_peers = [(((z + a) % 4) * 4 + (y + b) % 4, code) for a, b in steps]

    def z_peer(d):
        return (((z + d) % 4) * 4 + y, code)

    def y_peer(d):
        return (z * 4 + (y + d) % 4, code)

    def push(src, dst, send, recv, peer):
        pltpu.make_async_remote_copy(
            src_ref=src, dst_ref=dst, send_sem=send, recv_sem=recv,
            device_id=peer, device_id_type=MESH,
        ).start()

    for h in range(2):
        for p in range(NP):
            pltpu.make_async_copy(
                c_hbm.at[:, :, p, :, pl.ds(h * 128, 128)], s.at[h, :, p], c_sem.at[0]
            ).start()
    for r in range(4):
        pltpu.make_async_copy(x_hbm.at[r], e.at[7, :, pl.ds(r * 256, 256)], c_sem.at[1]).start()
    own_copy = pltpu.make_async_copy(c_hbm.at[z, y], cown, c_sem.at[2])
    own_copy.start()

    barrier = pltpu.get_barrier_semaphore()
    for d in (4, 3, 5, 2, 6, 1, 7):
        pl.semaphore_signal(barrier, inc=1, device_id=code_peers[d], device_id_type=MESH)
    for d in range(15):
        pl.semaphore_signal(barrier, inc=1, device_id=dp_peers[d], device_id_type=MESH)

    wait_bytes(s, c_sem.at[0])

    def prepare(n, carry):
        b, p = n // 2, n % 2
        half = pl.ds(p * (NP // 2), NP // 2)
        c0 = s[0, b, half].reshape(512, 128)
        c1 = s[1, b, half].reshape(512, 128)
        norm = jnp.sum(c0 * c0 + c1 * c1, axis=1, keepdims=True) * (-0.25 * LOG2E)
        rows = pl.ds(pl.multiple_of(p * 512, 512), 512)
        bias[b, rows, :] = jnp.broadcast_to(norm, (512, 128))
        for h, part in enumerate((c0, c1)):
            hi, lo = split(part * (0.5 * LOG2E))
            ccat[b, rows, h * 128:(h + 1) * 128] = hi
            ccat[b, rows, 256 + h * 128:256 + (h + 1) * 128] = lo
        return carry

    lax.fori_loop(0, 8, prepare, 0)
    wait_bytes(e.at[7], c_sem.at[1])

    def score(r, iq):
        raw = raws[iq % 2]
        lanes = slice(iq * 256, (iq + 1) * 256)
        xs = e[7, lanes, pl.ds(pl.multiple_of(r * 256, 256), 256)]
        xh, xl = split(xs)
        xcat[r, lanes, 0:256] = xh
        x8[r, lanes, :] = ((xs - xh.astype(F32)) * 256.0).astype(F8)
        x8[r, iq * 256 + 1024:iq * 256 + 1280, :] = xs.astype(F8)
        rhs = jnp.concatenate([xh, xl, xh], axis=1)
        top = None
        for slot in range(2):
            b = blocks[r, 0, slot]
            ch = ccat[b, :, 0:256]
            cl = ccat[b, :, 256:512]
            lhs = jnp.concatenate([ch, ch, cl], axis=1)
            bb = bias[b]
            value = lax.dot_general(lhs, rhs, NT, preferred_element_type=F32)
            value = value + jnp.concatenate([bb, bb], axis=1)
            raw[slot * 4:slot * 4 + 4] = value.reshape(4, 256, 256)
            peak = jnp.max(value.reshape(128, 8, 256), axis=0)
            peak = jnp.max(peak, axis=0, keepdims=True)
            if slot == 0:
                top = peak
            else:
                top = jnp.where(counts[r, 0] > 1, jnp.maximum(top, peak), top)
        rg0[r, code, :, lanes] = top

    def expo(r, iq):
        raw = raws[iq % 2]
        lanes = slice(iq * 256, (iq + 1) * 256)
        top = rg0[r, code, :, lanes]
        total = jnp.zeros((8, 256), F32)
        for slot in range(2):
            shift = top if slot == 0 else jnp.where(counts[r, 0] > 1, top, 3e38)
            for k in range(0, 1024, 256):
                rows = slice(k, k + 256)
                w = jnp.exp2(raw[slot * 4 + k // 256] - shift)
                e[r * 2 + slot, rows, lanes] = w
                total = total + jnp.sum(w.reshape(32, 8, 256), axis=0)
        rg0[r, code, :, 1024 + iq * 256:1280 + iq * 256] = jnp.sum(total, axis=0, keepdims=True)

    def send_first(r):
        for d in (4, 3, 5, 2, 6, 1, 7):
            push(rg0.at[r, code], rg0.at[r, code], r_send.at[0, r], r_recv.at[0, r], code_peers[d])

    score(0, 0)

    def row_first(r, carry):
        for iq in range(3):
            score(r, iq + 1)
            expo(r, iq)

        @pl.when(r == 0)
        def _():
            pl.semaphore_wait(barrier, 22)

        score(r + 1, 0)
        expo(r, 3)
        send_first(r)
        return carry

    lax.fori_loop(0, 3, row_first, 0)
    for iq in range(3):
        score(3, iq + 1)
        expo(3, iq)
    expo(3, 3)
    send_first(3)

    def col_block(r):
        g = gvec[r]
        for slot in range(2):
            def chunk(n, carry):
                k = pl.ds(pl.multiple_of(n * 256, 256), 256)
                w = e[r * 2 + slot, k, :] * g
                acc = w[:, 0:128]
                for j in range(1, 8):
                    acc = acc + w[:, j * 128:(j + 1) * 128]
                s[r // 2, (r % 2) * 2 + slot, pl.ds(n * 2, 2)] = acc.reshape(2, 4, Q, 128)
                return carry

            lax.fori_loop(0, 4, chunk, 0)

    def col_first(r, carry):
        wait_bytes(rg0.at[r, pl.ds(0, 7)], r_recv.at[0, r])
        tops = [rg0[r, j, :, 0:1024] for j in range(8)]
        best = functools.reduce(jnp.maximum, tops)
        total = jnp.zeros((1, 1024), F32)
        for j in range(8):
            total = total + jnp.exp2(tops[j] - best) * rg0[r, j, :, 1024:2048]
        mine = jnp.exp2(rg0[r, code, :, 0:1024] - best)
        alpha[r] = mine
        gvec[r] = mine / total
        col_block(r)
        return carry

    def factor(it, r):
        wait_bytes(rg.at[it, r, pl.ds(0, 7)], r_recv.at[it + 1, r])
        total = rg[it, r, 0]
        for j in range(1, 8):
            total = total + rg[it, r, j]
        gvec[r] = alpha[r] / total

    def col_next(r, carry):
        factor(0, r)
        col_block(r)
        return carry

    def row_next(it):
        def body(r, carry):
            acc = jnp.zeros((8, 1024), F32)
            for slot in range(2):
                b = blocks[r, 0, slot]

                def chunk(n, acc):
                    k = pl.ds(pl.multiple_of(n * 256, 256), 256)
                    w = e[r * 2 + slot, k, :] * repeat8(arep[b, k, :])
                    return acc + jnp.sum(w.reshape(32, 8, 1024), axis=0)

                acc = lax.fori_loop(0, 4, chunk, acc)
            rg[it, r, code] = jnp.sum(acc, axis=0, keepdims=True) * alpha[r]
            for d in (4, 3, 5, 2, 6, 1, 7):
                push(
                    rg.at[it, r, code], rg.at[it, r, code],
                    r_send.at[it + 1, r], r_recv.at[it + 1, r], code_peers[d],
                )
            return carry

        return body

    def has_slot(r, b):
        second = (blocks[r, 0, 1] == b) & (counts[r, 0] > 1)
        slot = jnp.where(second, 1, 0)
        has = second | (blocks[r, 0, 0] == b)
        return has, slot

    def next_a(it):
        def gather(b, carry):
            for p in range(NP):
                total = jnp.zeros((4, Q, 128), F32)
                for r in range(4):
                    has, slot = has_slot(r, b)
                    total = total + jnp.where(has, s[r // 2, (r % 2) * 2 + slot, p], 0.0)
                row = jnp.sum(total.reshape(128, 128).T, axis=0, keepdims=True)
                dg[it, b, dp, p:p + 1, :] = row
            for d in range(15):
                push(dg.at[it, b, dp], dg.at[it, b, dp], d_send.at[it, b], d_recv.at[it, b], dp_peers[d])
            return carry

        lax.fori_loop(0, 4, gather, 0)

        def lay(b, carry):
            wait_bytes(dg.at[it, b, pl.ds(0, 15)], d_recv.at[it, b])
            parts = [dg[it, b, j] for j in range(16)]
            while len(parts) > 1:
                parts = [parts[j] + parts[j + 1] for j in range(0, len(parts), 2)]
            a = 1.0 / (parts[0] + EPS)
            for j in range(8):
                arep[b, j * 128:(j + 1) * 128, :] = spread(a[j:j + 1, :])
            return carry

        lax.fori_loop(0, 4, lay, 0)

    lax.fori_loop(0, 4, col_first, 0)
    next_a(0)
    lax.fori_loop(0, 4, row_next(0), 0)
    lax.fori_loop(0, 4, col_next, 0)
    next_a(1)
    lax.fori_loop(0, 4, row_next(1), 0)

    def last_factor(r, carry):
        factor(1, r)
        return carry

    lax.fori_loop(0, 4, last_factor, 0)

    def part(p):
        rows = pl.ds(pl.multiple_of(p * CH, CH), CH)

        def one(r, carry):
            xh = xcat[r, :, 0:256]
            g = gvec[r]
            parts = []
            for slot in range(2):
                w = (e[r * 2 + slot, rows, :] * g) * repeat8(arep[blocks[r, 0, slot], rows, :])
                acc = w[:, 0:128]
                for j in range(1, 8):
                    acc = acc + w[:, j * 128:(j + 1) * 128]
                raw1[r * 2 + slot, 0:CH, 0:128] = acc
                hi = w.astype(BF16)
                lo = w - hi.astype(F32)
                parts.append((hi, jnp.concatenate([(w * 2.0**15).astype(F8), (lo * 2.0**23).astype(F8)], axis=1)))
            eh = jnp.concatenate([hi for hi, lo in parts], axis=0)
            el = jnp.concatenate([lo for hi, lo in parts], axis=0)
            value = jnp.dot(eh, xh, preferred_element_type=F32)
            value = value + jnp.dot(el, x8[r], preferred_element_type=F32) * 2.0**-23
            for slot in range(2):
                raw0[r * 2 + slot, 0:CH, :] = value[slot * CH:(slot + 1) * CH]
            return carry

        lax.fori_loop(0, 4, one, 0, unroll=4)
        for b in range(4):
            total = jnp.zeros((CH, 256), F32)
            mass = jnp.zeros((CH, 128), F32)
            for r in range(4):
                has, slot = has_slot(r, b)
                total = total + jnp.where(has, raw0[r * 2 + slot, 0:CH, :], 0.0)
                mass = mass + jnp.where(has, raw1[r * 2 + slot, 0:CH, 0:128], 0.0)
            s[0, b, p] = total[:, 0:128].reshape(4, Q, 128)
            s[1, b, p] = total[:, 128:256].reshape(4, Q, 128)
            my[p // 2, y, pl.ds((p % 2) * 4 + b, 1), :] = jnp.sum(mass.T, axis=0, keepdims=True)

    y_next, y_last, y_far = (y + 1) % 4, (y + 3) % 4, (y + 2) % 4
    z_next, z_last, z_far = (z + 1) % 4, (z + 3) % 4, (z + 2) % 4
    to_y_next, to_y_last = y_peer(1), y_peer(3)
    to_z_next, to_z_last = z_peer(1), z_peer(3)

    def far_parts(p, peers):
        push(s.at[0, pl.ds(0, 2), p, y_far], ya.at[p], p_send.at[0, p], p_recv.at[0, p], peers[0])
        push(s.at[1, z_far, p, pl.ds(0, 2)], za.at[p], p_send.at[2, p], p_recv.at[2, p], peers[1])
        push(s.at[0, pl.ds(2, 2), p, y_far], yb.at[p], p_send.at[1, p], p_recv.at[1, p], peers[2])
        push(s.at[1, z_far, p, pl.ds(2, 2)], zb.at[p], p_send.at[3, p], p_recv.at[3, p], peers[3])

    def next_y(p):
        push(s.at[0, :, p, y_next], yc.at[p], p_send.at[4, p], p_recv.at[4, p], to_y_next)

    def next_z(p):
        push(s.at[1, z_next, p], zc.at[p], p_send.at[6, p], p_recv.at[6, p], to_z_next)

    def last_y(p):
        push(s.at[0, :, p, y_last], yd.at[p], p_send.at[5, p], p_recv.at[5, p], to_y_last)

    def last_z(p):
        push(s.at[1, z_last, p], zd.at[p], p_send.at[7, p], p_recv.at[7, p], to_z_last)

    def step_one(p):
        @pl.when(p < NP - DIRECT)
        def _():
            far_parts(p, (to_y_next, to_z_next, to_y_last, to_z_last))

        @pl.when(p >= NP - DIRECT)
        def _():
            far_parts(p, (y_peer(2), z_peer(2), y_peer(2), z_peer(2)))
            next_y(p)
            next_z(p)
            last_y(p)
            last_z(p)

        @pl.when(p % 2 == 1)
        def _():
            for d in range(1, 4):
                push(my.at[p // 2, y], my.at[p // 2, y], m_send.at[0, p // 2], m_recv.at[0, p // 2], y_peer(d))

    def step_two(p):
        wait_bytes(ya.at[p], p_recv.at[0, p])
        s[0, 0:2, p, y_next] = s[0, 0:2, p, y_next] + ya[p]
        next_y(p)
        wait_bytes(za.at[p], p_recv.at[2, p])
        s[1, z_next, p, 0:2] = s[1, z_next, p, 0:2] + za[p]
        next_z(p)
        wait_bytes(yb.at[p], p_recv.at[1, p])
        s[0, 2:4, p, y_last] = s[0, 2:4, p, y_last] + yb[p]
        last_y(p)
        wait_bytes(zb.at[p], p_recv.at[3, p])
        s[1, z_last, p, 2:4] = s[1, z_last, p, 2:4] + zb[p]
        last_z(p)

    def step_three(p):
        wait_bytes(yc.at[p], p_recv.at[4, p])
        wait_bytes(yd.at[p], p_recv.at[5, p])

        @pl.when(p >= NP - DIRECT)
        def _():
            for n, ref in enumerate((ya, yb, za, zb)):
                wait_bytes(ref.at[p], p_recv.at[n, p])
            s[0, 0:2, p, y] = s[0, 0:2, p, y] + ya[p]
            s[0, 2:4, p, y] = s[0, 2:4, p, y] + yb[p]
            s[1, z, p, 0:2] = s[1, z, p, 0:2] + za[p]
            s[1, z, p, 2:4] = s[1, z, p, 2:4] + zb[p]

        s[0, :, p, y] = (s[0, :, p, y] + yc[p]) + yd[p]
        for d in range(1, 4):
            push(s.at[0, (z + d) % 4, p, y], u0.at[d - 1, p], p_send.at[8, p], p_recv.at[8, p], z_peer(d))
        wait_bytes(zc.at[p], p_recv.at[6, p])
        wait_bytes(zd.at[p], p_recv.at[7, p])
        s[1, z, p] = (s[1, z, p] + zc[p]) + zd[p]
        for d in range(1, 4):
            push(s.at[1, z, p, (y + d) % 4], u1.at[d - 1, p], p_send.at[9, p], p_recv.at[9, p], y_peer(d))

        @pl.when(p % 2 == 1)
        def _():
            n = p // 2
            wait_bytes(my.at[n, pl.ds(0, 3)], m_recv.at[0, n])
            mz[n, z] = (my[n, 0] + my[n, 1]) + (my[n, 2] + my[n, 3])
            for d in range(1, 4):
                push(mz.at[n, z], mz.at[n, z], m_send.at[1, n], m_recv.at[1, n], z_peer(d))

    own_copy.wait()

    def finish(p):
        @pl.when(p % 2 == 0)
        def _():
            n = p // 2
            wait_bytes(mz.at[n, pl.ds(0, 3)], m_recv.at[1, n])
            mass = (mz[n, 0] + mz[n, 1]) + (mz[n, 2] + mz[n, 3])
            mrep[1, 0:8, :] = mass

        mrep[0] = spread(mrep[1, pl.ds((p % 2) * 4 + z, 1), :])
        slack = EPS * arep[z, pl.ds(pl.multiple_of(p * CH + y * Q, Q), Q), :]
        a = 1.0 / (mrep[0, pl.ds(pl.multiple_of(y * Q, Q), Q), :] + slack)
        wait_bytes(u0.at[:, p], p_recv.at[8, p])
        wait_bytes(u1.at[:, p], p_recv.at[9, p])
        f0 = (s[0, z, p, y] + u0[0, p]) + (u0[1, p] + u0[2, p])
        f1 = (s[1, z, p, y] + u1[0, p]) + (u1[1, p] + u1[2, p])
        out_ref[p, :, 0:128] = (f0 + slack * cown[p, :, 0:128]) * a
        out_ref[p, :, 128:256] = (f1 + slack * cown[p, :, 128:256]) * a

    def final(n, carry):
        @pl.when(n < NP)
        def _():
            part(n)
            step_one(n)

        @pl.when((n >= LAG1) & (n < NP - DIRECT + LAG1))
        def _():
            step_two(n - LAG1)

        @pl.when((n >= LAG2) & (n < NP + LAG2))
        def _():
            step_three(n - LAG2)

        @pl.when(n >= LAG3)
        def _():
            finish(n - LAG3)

        return carry

    lax.fori_loop(0, NP + LAG3, final, 0)

    def drain_rows(r, carry):
        wait_bytes(rg0.at[r, pl.ds(0, 7)], r_send.at[0, r])
        wait_bytes(rg.at[0, r, pl.ds(0, 7)], r_send.at[1, r])
        wait_bytes(rg.at[1, r, pl.ds(0, 7)], r_send.at[2, r])
        wait_bytes(my.at[r, pl.ds(0, 3)], m_send.at[0, r])
        wait_bytes(mz.at[r, pl.ds(0, 3)], m_send.at[1, r])
        return carry

    lax.fori_loop(0, 4, drain_rows, 0)

    def drain_parts(p, carry):
        for n, ref in enumerate((ya, yb, za, zb, yc, yd, zc, zd)):
            wait_bytes(ref.at[p], p_send.at[n, p])
        wait_bytes(u0.at[:, p], p_send.at[8, p])
        wait_bytes(u1.at[:, p], p_send.at[9, p])
        return carry

    lax.fori_loop(0, NP, drain_parts, 0)
    for it in range(2):
        for b in range(4):
            wait_bytes(dg.at[it, b, pl.ds(0, 15)], d_send.at[it, b])


def local(vectors, codebook, cand_blocks, cand_counts):
    smem = pl.BlockSpec(memory_space=pltpu.SMEM)
    hbm = pl.BlockSpec(memory_space=pl.ANY)
    out = pl.pallas_call(
        kernel,
        out_shape=jax.ShapeDtypeStruct((NP, Q, 256), F32),
        in_specs=[smem, smem, hbm, hbm],
        out_specs=pl.BlockSpec(memory_space=pltpu.VMEM),
        scratch_shapes=[
            pltpu.VMEM((8, 1024, 1024), F32),
            pltpu.VMEM((2, 4, NP, 4, Q, 128), F32),
            pltpu.VMEM((4, 1024, 512), BF16),
            pltpu.VMEM((4, 1024, 256), BF16),
            pltpu.VMEM((4, 2048, 256), F8),
            pltpu.VMEM((4, 1024, 128), F32),
            pltpu.VMEM((4, 1024, 128), F32),
            pltpu.VMEM((8, 256, 256), F32),
            pltpu.VMEM((8, 256, 256), F32),
            pltpu.VMEM((NP, Q, 256), F32),
            pltpu.VMEM((4, 8, 1, 2048), F32),
            pltpu.VMEM((2, 4, 8, 1, 1024), F32),
            pltpu.VMEM((4, 1, 1024), F32),
            pltpu.VMEM((4, 1, 1024), F32),
            pltpu.VMEM((2, 4, 16, 8, 128), F32),
            pltpu.VMEM((4, 4, 8, 128), F32),
            pltpu.VMEM((4, 4, 8, 128), F32),
            pltpu.VMEM((2, 128, 128), F32),
            pltpu.VMEM((NP, 2, Q, 128), F32),
            pltpu.VMEM((NP, 2, Q, 128), F32),
            pltpu.VMEM((NP, 4, Q, 128), F32),
            pltpu.VMEM((NP, 4, Q, 128), F32),
            pltpu.VMEM((NP, 2, Q, 128), F32),
            pltpu.VMEM((NP, 2, Q, 128), F32),
            pltpu.VMEM((NP, 4, Q, 128), F32),
            pltpu.VMEM((NP, 4, Q, 128), F32),
            pltpu.VMEM((3, NP, Q, 128), F32),
            pltpu.VMEM((3, NP, Q, 128), F32),
            pltpu.SemaphoreType.DMA((3,)),
            pltpu.SemaphoreType.DMA((3, 4)),
            pltpu.SemaphoreType.DMA((3, 4)),
            pltpu.SemaphoreType.DMA((2, 4)),
            pltpu.SemaphoreType.DMA((2, 4)),
            pltpu.SemaphoreType.DMA((2, 4)),
            pltpu.SemaphoreType.DMA((2, 4)),
            pltpu.SemaphoreType.DMA((10, NP)),
            pltpu.SemaphoreType.DMA((10, NP)),
        ],
        compiler_params=pltpu.CompilerParams(
            collective_id=0, has_side_effects=True, vmem_limit_bytes=63 * 1024 * 1024,
        ),
    )(
        cand_blocks,
        cand_counts,
        vectors.reshape(4, 1024, 256),
        codebook.reshape(4, 4, NP, Q, 256),
    )
    return out.reshape(256, 256)


def solution(mesh):
    return jax.shard_map(
        local,
        mesh=mesh,
        in_specs=(P("dp", None), P("code", None), P("dp", "code", None), P("dp", "code")),
        out_specs=P(("code", "dp"), None),
        check_vma=False,
    )
```
